32 devices in a mesh: band: 2 (over x), patch: 16 (over z, y, core).
Axes of the slice: x: 2, y: 2, z: 4, core: 2. Of those that a mesh axis runs over, the one named last changes fastest.
Arguments:
- grid_feat: bfloat16 [8192, 474], P(('band', 'patch')), may hold values from -6 to 6
- enc_sender: int32 [12288], P(('band', 'patch')), may hold values from 0 to 255
- enc_patch: int32 [12288, 1], P(('band', 'patch')), may hold values from 0 to 15; in each aligned block of 384 rows (0 to 383, 384 to 767, ...) at most 32 rows name the same one
- enc_node: int32 [12288], P(('band', 'patch')), may hold values from 0 to 319
- enc_geo: bfloat16 [4, 12288], P(None, ('band', 'patch')), may hold values from -6 to 6
- mesh_nodes: bfloat16 [5120, 512], P('patch'), may hold values from -6 to 6
- mesh_edge: bfloat16 [8192, 512], P(('band', 'patch')), may hold values from -6 to 6
- mesh_send: int32 [8192], P(('band', 'patch')), may hold values from 0 to 575
- mesh_recv: int32 [8192], P(('band', 'patch')), may hold values from 0 to 319
- halo_rows: int32 [16, 256], P('patch'), may hold values from 0 to 319
- grid_in: bfloat16 [474, 512], replicated, may hold values from -0.25 to 0.25
- grid_out: bfloat16 [512, 512], replicated, may hold values from -0.25 to 0.25
- geo_weight: bfloat16 [4, 512], replicated, may hold values from -3 to 3
- enc_edge_w: bfloat16 [3, 512, 512], replicated, may hold values from -0.25 to 0.25
- enc_node_w: bfloat16 [3, 512, 512], replicated, may hold values from -0.25 to 0.25
- proc_edge_w: bfloat16 [4, 512, 512], replicated, may hold values from -0.25 to 0.25
- proc_node_w: bfloat16 [3, 512, 512], replicated, may hold values from -0.25 to 0.25
Outputs:
- mesh_two: bfloat16 [5120, 512], P('patch')
- edge_out: bfloat16 [8192, 512], P(('band', 'patch'))
The draws below stay inside these ranges and needn't reach their ends.
Inputs may be any that keep to these rules, and one draw needn't show every extreme that they name: `enc_sender`: row among the 256 grid rows of the device that holds the edge. `enc_patch`: among the 384 edge rows of one device no patch is named more than 32 times; some patch exactly 32 times. `mesh_send`: values from 320 on name rows received from other patches, as in the reference program. `halo_rows`: row q holds, in blocks of 16, the rows of patch q sent to patches 0, 1,.
All inputs are finite; a program needn't handle non-finite values.
Results may differ from the reference program's by a relative error of at most 0.017.
Values may be sent and summed in bfloat16 or wider, within the bound.
No kernel may reach another device: no remote copies, remote signals or barrier semaphores. Data moves between devices by JAX's collectives and lax.ppermute only.
A program may use at most 64 MiB of HBM per device.

```python
import math
import jax
import jax.numpy as jnp
import numpy as np
from jax import lax

D = 512
C_IN = 474
G_DEV = 256
E_DEV = 384
M_DEV = 320
ME_DEV = 256
HALO_DEV = 256
CAP = 32
H_PEER = 16
GRID = 8192
EDGES = 12288
MESH = 5120
MEDGES = 8192
N_BAND = 2
N_PATCH = 16


def touch_ends(drawn, key, smallest, high):
    longest = drawn.shape.index(max(drawn.shape))
    spots = []
    for shift in (0, 1):
        where = [jax.random.randint(jax.random.fold_in(key, axis), (), 0, length) for axis, length in enumerate(drawn.shape)]
        where[longest] = (where[longest] + shift) % drawn.shape[longest]
        spots.append(tuple(where))
    return drawn.at[spots[0]].set(smallest).at[spots[1]].set(high)


def block_scale(own_key, dims, split, least, largest):
    level = 1.0
    for position, blocks in split:
        draws = jax.random.uniform(jax.random.fold_in(jax.random.fold_in(own_key, 6), position), (blocks,), jnp.float32, least / len(split), largest / len(split))
        level = level * jnp.repeat(jnp.exp(draws), dims[position] // blocks).reshape((-1,) + (1,) * (len(dims) - 1 - position))
    return level


def shared_out(rng, own, number, rows, count, top, limit, skew):
    ranking = jax.random.permutation(rng, count)
    crowded, common = shares(count, rows * top, limit, skew, True), shares(count, rows * top, limit, skew, False)
    places = jnp.arange(count)

    def named(lengths, turn):
        used = int((lengths > 0).sum())
        fixed = max(1, used // 4)
        passed = fixed + (places - fixed + turn * (used - fixed)) % max(1, count - fixed)
        return jnp.zeros((count,), jnp.int32).at[ranking[jnp.where(places < fixed, places, passed)]].set(jnp.asarray(lengths, jnp.int32))

    lengths = jnp.where(number % 4 == 0, named(crowded, number // 4), named(common, number - number // 4 - 1))
    mixed = jax.random.permutation(jax.random.fold_in(own, 3), count)
    donor, taker = mixed[0:count // 2 * 2:2], mixed[1:count // 2 * 2:2]
    slack = jnp.minimum(lengths[donor] - 1, limit - lengths[taker]) // 2
    slack = jnp.where((donor == ranking[0]) | (taker == ranking[0]) | (lengths[taker] == 0), 0, jnp.maximum(slack, 0))
    passed = jax.random.randint(jax.random.fold_in(own, 4), (count // 2,), 0, 1 << 20) % (slack + 1)
    lengths = lengths.at[donor].add(-passed).at[taker].add(passed)
    items = jnp.searchsorted(jnp.cumsum(lengths), jnp.arange(rows * top), side="right").astype(jnp.int32)
    table = items.reshape(top, rows).T
    table = table[jax.random.permutation(jax.random.fold_in(own, 1), rows)]
    turn = jax.random.randint(jax.random.fold_in(own, 2), (rows, 1), 0, top)
    return jnp.take_along_axis(table, (jnp.arange(top)[None, :] + turn) % top, axis=1)


def shares(count, total, bound, skew, full):
    weights = [(1 << 20) // math.isqrt(standing ** skew) + 1 for standing in range(1, count + 1)]
    largest = bound if full else min(bound, max(-(-total // count), total * weights[0] // sum(weights)))
    least = 1 if total - largest >= count - 1 else 0
    holding, spare = [largest] + [least] * (count - 1), total - largest - least * (count - 1)
    while spare > 0:
        candidates = [i for i in range(1, count) if holding[i] < largest] or [i for i in range(1, count) if holding[i] < bound]
        mass, budget = sum([weights[i] for i in candidates]), spare
        for i in candidates:
            addition = min(bound - holding[i], max(1, budget * weights[i] // mass), spare)
            holding[i] = holding[i] + addition
            spare = spare - addition
    return np.array(holding)


def scatter_about(rng, dims, width, limit, cuts=(), kind=jnp.bfloat16):
    gain = block_scale(rng, dims, cuts, -0.22, 0.18) if cuts else 1.0
    drawn = jax.random.normal(rng, dims, jnp.float32) * width * gain
    return jnp.minimum(jnp.maximum(drawn, -limit), limit).astype(kind)


def setup_inputs(seed: int = 0) -> dict:
    splits = jax.random.split(jax.random.key(seed), 18)
    grid_feat = scatter_about(splits[0], (GRID, C_IN), 1.0, 6.0, ((0, 32),))
    enc_sender = touch_ends(jax.random.randint(splits[1], (EDGES,), 0, G_DEV), jax.random.fold_in(splits[1], 1), 0, G_DEV - 1).astype(jnp.int32)
    enc_patch_keys = jax.random.split(jax.random.fold_in(splits[2], 1), EDGES // E_DEV)
    enc_patch_turns = jax.random.permutation(jax.random.fold_in(splits[2], 3), EDGES // E_DEV)
    enc_patch = jax.vmap(lambda own, number: shared_out(jax.random.fold_in(splits[2], 2), own, number, E_DEV, N_PATCH, 1, CAP, 1))(enc_patch_keys, enc_patch_turns).reshape((EDGES, 1))
    enc_node = touch_ends(jax.random.randint(splits[3], (EDGES,), 0, M_DEV), jax.random.fold_in(splits[3], 1), 0, M_DEV - 1).astype(jnp.int32)
    enc_geo = scatter_about(splits[4], (4, EDGES), 1.0, 6.0, ((1, 32),))
    mesh_nodes = scatter_about(splits[5], (MESH, D), 1.0, 6.0, ((0, 16),))
    mesh_edge = scatter_about(splits[6], (MEDGES, D), 1.0, 6.0, ((0, 32),))
    mesh_send = touch_ends(jax.random.randint(splits[7], (MEDGES,), 0, M_DEV + HALO_DEV), jax.random.fold_in(splits[7], 1), 0, (M_DEV + HALO_DEV) - 1).astype(jnp.int32)
    mesh_recv = touch_ends(jax.random.randint(splits[8], (MEDGES,), 0, M_DEV), jax.random.fold_in(splits[8], 1), 0, M_DEV - 1).astype(jnp.int32)
    halo_rows = touch_ends(jax.random.randint(splits[9], (N_PATCH, HALO_DEV), 0, M_DEV), jax.random.fold_in(splits[9], 1), 0, M_DEV - 1).astype(jnp.int32)
    grid_in = scatter_about(splits[10], (C_IN, D), C_IN ** -0.5, 0.25)
    grid_out = scatter_about(splits[11], (D, D), D ** -0.5, 0.25)
    geo_weight = scatter_about(splits[12], (4, D), 4 ** -0.5, 3.0)
    enc_edge_w = scatter_about(splits[13], (3, D, D), D ** -0.5, 0.25)
    enc_node_w = scatter_about(splits[14], (3, D, D), D ** -0.5, 0.25)
    proc_edge_w = scatter_about(splits[15], (4, D, D), D ** -0.5, 0.25)
    proc_node_w = scatter_about(splits[16], (3, D, D), D ** -0.5, 0.25)
    return {"grid_feat": grid_feat, "enc_sender": enc_sender, "enc_patch": enc_patch, "enc_node": enc_node, "enc_geo": enc_geo, "mesh_nodes": mesh_nodes, "mesh_edge": mesh_edge, "mesh_send": mesh_send, "mesh_recv": mesh_recv, "halo_rows": halo_rows, "grid_in": grid_in, "grid_out": grid_out, "geo_weight": geo_weight, "enc_edge_w": enc_edge_w, "enc_node_w": enc_node_w, "proc_edge_w": proc_edge_w, "proc_node_w": proc_node_w}


def norm_rows(values_in):
    average = lax.optimization_barrier(jnp.mean(values_in, axis=-1, keepdims=True))
    centred = values_in - average
    spread = lax.optimization_barrier(jnp.mean(centred * centred, axis=-1, keepdims=True))
    return centred * lax.rsqrt(spread + 1e-05)

def network_tail(preact, out_weight):
    hidden = jax.nn.silu(preact).astype(jnp.bfloat16)
    return norm_rows(jnp.dot(hidden, out_weight, preferred_element_type=jnp.float32))

def update_rows(node_rows, running, weights):
    preact = jnp.dot(node_rows, weights[0], preferred_element_type=jnp.float32) + jnp.dot(running.astype(jnp.bfloat16), weights[1], preferred_element_type=jnp.float32)
    return (node_rows.astype(jnp.float32) + network_tail(preact, weights[2])).astype(jnp.bfloat16)

def reference(grid_feat, enc_sender, enc_patch, enc_node, enc_geo, mesh_nodes, mesh_edge, mesh_send, mesh_recv, halo_rows, grid_in, grid_out, geo_weight, enc_edge_w, enc_node_w, proc_edge_w, proc_node_w):

    def embed_grid(pieces):
        hidden = jax.nn.silu(jnp.dot(pieces, grid_in, preferred_element_type=jnp.float32)).astype(jnp.bfloat16)
        latent = norm_rows(jnp.dot(hidden, grid_out, preferred_element_type=jnp.float32)).astype(jnp.bfloat16)
        return jnp.dot(latent, enc_edge_w[0], preferred_element_type=jnp.float32)
    sender_proj = lax.map(embed_grid, grid_feat.reshape(N_BAND, -1, C_IN)).reshape(GRID, D)
    edge_ids = jnp.arange(EDGES, dtype=jnp.int32)
    senders = enc_sender.astype(jnp.int32) + edge_ids // E_DEV * G_DEV
    receivers = enc_patch[:, 0].astype(jnp.int32) * M_DEV + enc_node.astype(jnp.int32)
    recv_proj = jnp.dot(mesh_nodes, enc_edge_w[1], preferred_element_type=jnp.float32)
    geo_blocks = enc_geo.reshape(4, N_BAND, -1).transpose(1, 0, 2)

    def encode_band(running, pieces):
        send_rows, geo_block, recv_rows = pieces
        geo_term = lax.dot_general(geo_block, geo_weight, (((0,), (0,)), ((), ())), preferred_element_type=jnp.float32)
        send_term = (sender_proj[send_rows] + geo_term).astype(jnp.bfloat16)
        preact = send_term.astype(jnp.float32) + recv_proj[recv_rows]
        message = network_tail(preact, enc_edge_w[2])
        return (running + jax.ops.segment_sum(message, recv_rows, num_segments=MESH), None)
    enc_agg, _ = lax.scan(encode_band, jnp.zeros((MESH, D), jnp.float32), (senders.reshape(N_BAND, -1), geo_blocks, receivers.reshape(N_BAND, -1)))
    mesh_one = update_rows(mesh_nodes, enc_agg, enc_node_w)
    sent_proj = jnp.dot(mesh_one, proc_edge_w[1], preferred_element_type=jnp.float32).astype(jnp.bfloat16)
    recv_two = jnp.dot(mesh_one, proc_edge_w[2], preferred_element_type=jnp.float32)
    mesh_ids = jnp.arange(MEDGES, dtype=jnp.int32)
    patch_of = mesh_ids // ME_DEV % N_PATCH
    sender_local = mesh_send.astype(jnp.int32)
    ghost_index = jnp.maximum(sender_local - M_DEV, 0)
    source = ghost_index // H_PEER
    within = ghost_index % H_PEER
    far_rows = halo_rows.reshape(-1).astype(jnp.int32)[source * HALO_DEV + patch_of * H_PEER + within]
    node_index = jnp.where(sender_local < M_DEV, patch_of * M_DEV + sender_local, source * M_DEV + far_rows)
    target = patch_of * M_DEV + mesh_recv.astype(jnp.int32)

    def process_band(running, pieces):
        edge_block, node_block, target_block = pieces
        preact = jnp.dot(edge_block, proc_edge_w[0], preferred_element_type=jnp.float32) + sent_proj[node_block].astype(jnp.float32) + recv_two[target_block]
        updated = edge_block.astype(jnp.float32) + network_tail(preact, proc_edge_w[3])
        return (running + jax.ops.segment_sum(updated, target_block, num_segments=MESH), updated.astype(jnp.bfloat16))
    proc_agg, edge_blocks = lax.scan(process_band, jnp.zeros((MESH, D), jnp.float32), (mesh_edge.reshape(N_BAND, -1, D), node_index.reshape(N_BAND, -1), target.reshape(N_BAND, -1)))
    mesh_two = update_rows(mesh_one, proc_agg, proc_node_w)
    return (mesh_two, edge_blocks.reshape(MEDGES, D))
```

```python
import functools

import jax
import jax.numpy as jnp
from jax import lax
from jax.experimental import pallas as pl
from jax.experimental.pallas import tpu as pltpu
from jax.sharding import PartitionSpec as P

F32 = jnp.float32
BF16 = jnp.bfloat16
LANES = 128
RADIX = 32


def dot_nn(left, right):
    return jnp.dot(left, right, preferred_element_type=F32)


def dot_nt(left, right):
    return lax.dot_general(left, right, (((1,), (1,)), ((), ())), preferred_element_type=F32)


def dot_tn(left, right):
    return lax.dot_general(left, right, (((0,), (0,)), ((), ())), preferred_element_type=F32)


def as_onehot(hits):
    return jnp.where(hits, 1.0, 0.0).astype(BF16)


def rows_equal(row_count, names):
    rows = lax.broadcasted_iota(jnp.int32, (row_count, names.shape[1]), 0)
    return as_onehot(rows == names)


def norm_rows(values_in):
    average = jnp.mean(values_in, axis=-1, keepdims=True)
    centred = values_in - average
    spread = jnp.mean(centred * centred, axis=-1, keepdims=True)
    return centred * lax.rsqrt(spread + 1e-05)


def silu(values_in):
    return values_in * jax.nn.sigmoid(values_in)


def tail(preact, out_weight):
    return norm_rows(dot_nn(silu(preact).astype(BF16), out_weight))


def embed_kernel(
    feat_ref, sender_ref, patch_ref, node_ref, geo_ref, in_ref, out_ref, geo_w_ref, edge_w_ref, box_ref
):
    peers, box_rows, _ = box_ref.shape
    edges = sender_ref.shape[1]
    grid_rows = feat_ref.shape[1]
    pieces = edge_w_ref.shape[2] // LANES
    capacity = 4 * edges // (3 * peers)
    slots = peers * capacity
    me = lax.axis_index("patch")
    patch = patch_ref[...]
    named = lax.broadcasted_iota(jnp.int32, (peers, edges), 0) == patch
    named_f = jnp.where(named, 1.0, 0.0)
    earlier = as_onehot(
        lax.broadcasted_iota(jnp.int32, (edges, edges), 0)
        < lax.broadcasted_iota(jnp.int32, (edges, edges), 1)
    )
    before = dot_nn(named_f.astype(BF16), earlier)
    rank = jnp.sum(named_f * before, axis=0, keepdims=True).astype(jnp.int32)
    place = rows_equal(slots, patch * capacity + rank)
    source = rows_equal(grid_rows, sender_ref[...])
    pick = dot_nt(place, source).astype(BF16)
    geo = dot_nt(place, geo_ref[...]).astype(BF16)

    hidden = silu(dot_tn(feat_ref[...], in_ref[...])).astype(BF16)
    latent = norm_rows(dot_nn(hidden, out_ref[...])).astype(BF16)
    rows = dot_nn(pick, latent).astype(BF16)
    term = dot_nn(rows, edge_w_ref[0]) + dot_nn(geo, geo_w_ref[...])
    for piece in range(pieces):
        box_ref[:, piece * capacity : (piece + 1) * capacity, :] = (
            term[:, piece * LANES : (piece + 1) * LANES].reshape(peers, capacity, LANES).astype(BF16)
        )

    address = node_ref[...] + 1
    first = me * capacity
    lane = rows_equal(LANES, rank + lax.rem(first, LANES))
    high = dot_nt((named_f * (address // RADIX).astype(F32)).astype(BF16), lane)
    low = dot_nt((named_f * lax.rem(address, RADIX).astype(F32)).astype(BF16), lane)
    extra = box_rows - pieces * capacity
    row = lax.broadcasted_iota(jnp.int32, (peers, extra, LANES), 1)
    mine = first // LANES
    words = jnp.where(
        row == mine,
        high[:, None, :],
        jnp.where(row == extra // 2 + mine, low[:, None, :], 0.0),
    )
    box_ref[:, pieces * capacity :, :] = words.astype(BF16)


def shadow_kernel(node_ref, halo_ref, edge_w_ref, node_w_ref, recv_ref, pre_ref, halo_hot_ref):
    nodes = node_ref[...]
    recv_ref[...] = dot_nn(nodes, edge_w_ref[0]).astype(BF16)
    pre_ref[...] = dot_nn(nodes, node_w_ref[0])
    halo_hot_ref[...] = rows_equal(nodes.shape[0], halo_ref[...]).T


def edge_shadow_kernel(*refs, count):
    edge_refs, send_refs, recv_refs = refs[:count], refs[count : 2 * count], refs[2 * count : 3 * count]
    edge_w_ref, edges_ref, pre_ref, ends_ref, far_ref, target_ref = refs[3 * count :]
    size = edge_refs[0].shape[0]
    mesh_rows = target_ref.shape[0]
    far_rows = far_ref.shape[1]
    for part in range(count):
        rows = slice(part * size, (part + 1) * size)
        if count == 2:
            keep = lax.axis_index("band") == part
            edges = jnp.where(keep, edge_refs[0][...], edge_refs[1][...])
            send = jnp.where(keep, send_refs[0][...], send_refs[1][...])
            recv = jnp.where(keep, recv_refs[0][...], recv_refs[1][...])
        else:
            edges, send, recv = edge_refs[0][...], send_refs[0][...], recv_refs[0][...]
        edges_ref[rows, :] = edges
        pre_ref[rows, :] = dot_nn(edges, edge_w_ref[0])
        receiver = rows_equal(mesh_rows, recv)
        target_ref[:, rows] = receiver
        near = rows_equal(mesh_rows, send)
        far = rows_equal(far_rows, send - mesh_rows)
        ends_ref[rows, :mesh_rows] = near.T
        ends_ref[rows, mesh_rows:] = receiver.T
        far_ref[rows, :] = far.T


def message_kernel(box_ref, recv_ref, out_w_ref, total_ref, *, capacity):
    peers = box_ref.shape[0]
    mesh_rows, width = recv_ref.shape
    pieces = width // LANES
    words = jnp.sum(box_ref[:, pieces * capacity :, :].astype(F32), axis=0)
    half = words.shape[0] // 2
    slots = peers * capacity
    hot = []
    for group in range(slots // LANES):
        name = words[group : group + 1] * float(RADIX) + words[half + group : half + group + 1] - 1.0
        hot.append(rows_equal(mesh_rows, name.astype(jnp.int32)))
    hot = jnp.concatenate(hot, axis=1)
    terms = jnp.concatenate(
        [
            box_ref[:, piece * capacity : (piece + 1) * capacity, :].astype(F32).reshape(slots, LANES)
            for piece in range(pieces)
        ],
        axis=1,
    )
    message = tail(terms + dot_tn(hot, recv_ref[...]), out_w_ref[0])
    total_ref[...] = dot_nn(hot, message.astype(BF16)).astype(BF16)


def add_up(refs):
    total = refs[0][...].astype(F32)
    for ref in refs[1:]:
        total = total + ref[...].astype(F32)
    return total.astype(BF16)


def mesh_kernel(*refs, count):
    total = add_up(refs[:count])
    node_ref, pre_ref, sum_w_ref, out_w_ref, sent_w_ref, halo_hot_ref, one_ref, box_ref = refs[count:]
    preact = pre_ref[...] + dot_nn(total, sum_w_ref[0])
    one = (node_ref[...].astype(F32) + tail(preact, out_w_ref[0])).astype(BF16)
    one_ref[...] = one
    rows = dot_nn(halo_hot_ref[...], one).astype(BF16)
    box_ref[...] = dot_nn(rows, sent_w_ref[0]).astype(BF16)


def local_kernel(one_ref, pre_ref, ends_ref, sent_w_ref, recv_w_ref, node_w_ref, out_ref, node_pre_ref):
    one = one_ref[...]
    sent = dot_nn(one, sent_w_ref[0]).astype(BF16)
    recv = dot_nn(one, recv_w_ref[0]).astype(BF16)
    out_ref[...] = pre_ref[...] + dot_nn(ends_ref[...], jnp.concatenate([sent, recv], axis=0))
    node_pre_ref[...] = dot_nn(one, node_w_ref[0])


def edge_values(ghost_ref, far_ref, pre_ref, edges_ref, out_w_ref):
    preact = pre_ref[...] + dot_nn(far_ref[...], ghost_ref[...])
    return edges_ref[...].astype(F32) + tail(preact, out_w_ref[0])


def node_values(total, one_ref, node_pre_ref, sum_w_ref, out_w_ref):
    preact = node_pre_ref[...] + dot_nn(total, sum_w_ref[0])
    return (one_ref[...].astype(F32) + tail(preact, out_w_ref[0])).astype(BF16)


def edge_node_kernel(
    ghost_ref, far_ref, pre_ref, edges_ref, edge_w_ref, target_ref,
    one_ref, node_pre_ref, sum_w_ref, out_w_ref, edge_out_ref, two_ref, held_ref,
):
    held_ref[...] = edge_values(ghost_ref, far_ref, pre_ref, edges_ref, edge_w_ref).astype(BF16)
    size = edge_out_ref.shape[0]
    first = pl.multiple_of(lax.axis_index("band") * size, size)
    edge_out_ref[...] = held_ref[pl.ds(first, size), :]
    total = dot_nn(target_ref[...], held_ref[...]).astype(BF16)
    two_ref[...] = node_values(total, one_ref, node_pre_ref, sum_w_ref, out_w_ref)


def edge_kernel(ghost_ref, far_ref, pre_ref, edges_ref, edge_w_ref, target_ref, edge_out_ref, total_ref):
    held = edge_values(ghost_ref, far_ref, pre_ref, edges_ref, edge_w_ref).astype(BF16)
    edge_out_ref[...] = held
    total_ref[...] = dot_nn(target_ref[...], held).astype(BF16)


def node_kernel(total_ref, one_ref, node_pre_ref, sum_w_ref, out_w_ref, two_ref):
    two_ref[...] = node_values(total_ref[...], one_ref, node_pre_ref, sum_w_ref, out_w_ref)


def call(kernel, outs, operands, flops, scratch=()):
    specs, arrays, moved = [], [], 0
    for operand in operands:
        if isinstance(operand, tuple):
            array, index = operand
            block = (1,) + array.shape[1:]
            specs.append(pl.BlockSpec(block, lambda i, index=index: (index, 0, 0)))
            moved += array.size // array.shape[0] * 2
        else:
            array = operand
            specs.append(pl.BlockSpec(array.shape, lambda i, rank=array.ndim: (0,) * rank))
            moved += array.size * array.dtype.itemsize
        arrays.append(array)
    return pl.pallas_call(
        kernel,
        grid=(1,),
        in_specs=specs,
        out_specs=[pl.BlockSpec(o.shape, lambda i, rank=len(o.shape): (0,) * rank) for o in outs],
        out_shape=outs,
        scratch_shapes=scratch,
        compiler_params=pltpu.CompilerParams(vmem_limit_bytes=32 * 1024 * 1024),
        cost_estimate=pl.CostEstimate(flops=flops, bytes_accessed=moved, transcendentals=0),
    )(*arrays)


def shape(dims, dtype=BF16):
    return jax.ShapeDtypeStruct(dims, dtype)


def per_device(
    grid_feat,
    enc_sender,
    enc_patch,
    enc_node,
    enc_geo,
    mesh_nodes,
    mesh_edge,
    mesh_send,
    mesh_recv,
    halo_rows,
    grid_in,
    grid_out,
    geo_weight,
    enc_edge_w,
    enc_node_w,
    proc_edge_w,
    proc_node_w,
):
    bands, peers = lax.axis_size("band"), lax.axis_size("patch")
    mesh_count, width = mesh_nodes.shape
    edge_count, medge_count = enc_sender.shape[0], mesh_edge.shape[0]
    halo_count = halo_rows.shape[1]
    capacity = 4 * edge_count // (3 * peers)
    slots = peers * capacity
    pieces = width // LANES
    address_rows = 2 * (slots // LANES)
    paired = bands == 2
    other = [(0, 1), (1, 0)]
    unit = 2 * width * width

    def band_sum(partial_value):
        share = lax.psum_scatter(partial_value, "band", scatter_dimension=0, tiled=True)
        return lax.all_gather(share, "band", axis=0, tiled=True)

    send_row, recv_row = mesh_send.reshape(1, -1), mesh_recv.reshape(1, -1)
    edge_parts, send_parts, recv_parts = [mesh_edge], [send_row], [recv_row]
    if paired:
        edge_parts.append(lax.ppermute(mesh_edge, "band", other))
        names = lax.ppermute(jnp.concatenate([send_row, recv_row], axis=0), "band", other)
        send_parts.append(names[0:1])
        recv_parts.append(names[1:2])
    count = len(edge_parts)
    edge_total = count * medge_count

    (outbox,) = call(
        embed_kernel,
        [shape((peers, pieces * capacity + address_rows, LANES))],
        [
            grid_feat.T,
            enc_sender.reshape(1, -1),
            enc_patch.reshape(1, -1),
            enc_node.reshape(1, -1),
            enc_geo,
            grid_in,
            grid_out,
            geo_weight,
            (enc_edge_w, 0),
        ],
        unit * 1500,
    )
    inbox = lax.all_to_all(outbox, "patch", split_axis=0, concat_axis=0, tiled=True)

    recv_proj, node_pre, halo_hot = call(
        shadow_kernel,
        [shape((mesh_count, width)), shape((mesh_count, width), F32), shape((halo_count, mesh_count))],
        [mesh_nodes, halo_rows, (enc_edge_w, 1), (enc_node_w, 0)],
        unit * 640,
    )
    edges, edge_pre, ends, far, target = call(
        functools.partial(edge_shadow_kernel, count=count),
        [
            shape((edge_total, width)),
            shape((edge_total, width), F32),
            shape((edge_total, 2 * mesh_count)),
            shape((edge_total, halo_count)),
            shape((mesh_count, edge_total)),
        ],
        edge_parts + send_parts + recv_parts + [(proc_edge_w, 0)],
        unit * edge_total,
    )

    (partial_value,) = call(
        functools.partial(message_kernel, capacity=capacity),
        [shape((mesh_count, width))],
        [inbox, recv_proj, (enc_edge_w, 2)],
        unit * 1200,
    )
    if paired:
        totals = [partial_value, lax.ppermute(partial_value, "band", other)]
    else:
        totals = [band_sum(partial_value)]
    mesh_one, halo_box = call(
        functools.partial(mesh_kernel, count=len(totals)),
        [shape((mesh_count, width)), shape((halo_count, width))],
        totals
        + [mesh_nodes, node_pre, (enc_node_w, 1), (enc_node_w, 2), (proc_edge_w, 1), halo_hot],
        unit * 1000,
    )
    ghosts = lax.all_to_all(
        halo_box.reshape(peers, -1, width), "patch", split_axis=0, concat_axis=0, tiled=True
    ).reshape(halo_count, width)
    edge_pre, node_pre = call(
        local_kernel,
        [shape((edge_total, width), F32), shape((mesh_count, width), F32)],
        [mesh_one, edge_pre, ends, (proc_edge_w, 1), (proc_edge_w, 2), (proc_node_w, 0)],
        unit * 1500,
    )
    edge_operands = [ghosts, far, edge_pre, edges, (proc_edge_w, 3), target]
    node_operands = [mesh_one, node_pre, (proc_node_w, 1), (proc_node_w, 2)]
    if paired:
        edge_out, mesh_two = call(
            edge_node_kernel,
            [shape((medge_count, width)), shape((mesh_count, width))],
            edge_operands + node_operands,
            unit * 1500,
            scratch=[pltpu.VMEM((edge_total, width), BF16)],
        )
    else:
        edge_out, partial_two = call(
            edge_kernel,
            [shape((medge_count, width)), shape((mesh_count, width))],
            edge_operands,
            unit * 800,
        )
        (mesh_two,) = call(
            node_kernel,
            [shape((mesh_count, width))],
            [band_sum(partial_two)] + node_operands,
            unit * 640,
        )
    return (mesh_two, edge_out)


def solution(mesh):
    both = ("band", "patch")
    in_specs = (
        P(both, None),
        P(both),
        P(both, None),
        P(both),
        P(None, both),
        P("patch", None),
        P(both, None),
        P(both),
        P(both),
        P("patch", None),
        P(),
        P(),
        P(),
        P(),
        P(),
        P(),
        P(),
    )
    out_specs = (P("patch", None), P(both, None))
    return jax.shard_map(
        per_device, mesh=mesh, in_specs=in_specs, out_specs=out_specs, check_vma=False
    )
```

```python
import functools
import math

import jax
import jax.numpy as jnp
from jax import lax
from jax.experimental import pallas as pl
from jax.experimental.pallas import tpu as pltpu
from jax.sharding import PartitionSpec as P

F32 = jnp.float32
BF16 = jnp.bfloat16
LANES = 128
RADIX = 32


def dot_nn(left, right):
    return jnp.dot(left, right, preferred_element_type=F32)


def dot_nt(left, right):
    return lax.dot_general(left, right, (((1,), (1,)), ((), ())), preferred_element_type=F32)


def dot_tn(left, right):
    return lax.dot_general(left, right, (((0,), (0,)), ((), ())), preferred_element_type=F32)


def as_onehot(hits):
    return jnp.where(hits, 1.0, 0.0).astype(BF16)


def rows_equal(row_count, names):
    rows = lax.broadcasted_iota(jnp.int32, (row_count, names.shape[1]), 0)
    return as_onehot(rows == names)


def norm_rows(values_in):
    average = jnp.mean(values_in, axis=-1, keepdims=True)
    centred = values_in - average
    spread = jnp.mean(centred * centred, axis=-1, keepdims=True)
    return centred * lax.rsqrt(spread + 1e-05)


def silu(values_in):
    return values_in * jax.nn.sigmoid(values_in)


def tail(preact, out_weight):
    return norm_rows(dot_nn(silu(preact).astype(BF16), out_weight))


class Arriving:
    def __init__(self, source, held, sem):
        self.held, self.copy, self.waited = held, pltpu.make_async_copy(source, held, sem), False
        self.copy.start()

    def ref(self):
        if not self.waited:
            self.copy.wait()
            self.waited = True
        return self.held

    def __call__(self):
        return self.ref()[...]


class Present:
    def __init__(self, held):
        self.held = held

    def ref(self):
        return self.held

    def __call__(self):
        return self.held[...]


class Leaving:
    def __init__(self, held, target=None, sems=None):
        self.held, self.target, self.sems, self.copies = held, target, sems, []
        self.shape = held.shape

    def send(self, first, count):
        if self.target is not None:
            rows = pl.ds(first, count)
            copy = pltpu.make_async_copy(
                self.held.at[rows], self.target.at[rows], self.sems.at[len(self.copies)]
            )
            copy.start()
            self.copies.append(copy)

    def put(self, value, first=0):
        self.held[first : first + value.shape[0]] = value
        self.send(first, value.shape[0])


class Far:
    def __init__(self, array, index=None, count=None):
        self.array, self.index, self.count = array, index, count
        self.shape = array.shape
        if index is not None:
            self.shape = array.shape[1:] if count is None else (count,) + array.shape[1:]

    def source(self, ref):
        if self.index is None:
            return ref
        return ref.at[self.index if self.count is None else pl.ds(self.index, self.count)]


PARTS = 4
BIG, MID, SMALL = 60, 48, 12


def call(body, outs, operands, flops, far_outs=False, room=SMALL):
    n_in, n_out = len(operands), len(outs)
    far_in = [isinstance(operand, Far) for operand in operands]
    arrays = [operand.array if away else operand for operand, away in zip(operands, far_in)]
    moved = sum(math.prod(o.shape) * a.dtype.itemsize for o, a in zip(operands, arrays))

    def kernel(*refs):
        given, results, scratch = refs[:n_in], refs[n_in : n_in + n_out], list(refs[n_in + n_out : -2])
        in_sems, out_sems = refs[-2:]
        arriving = []
        for i, (ref, operand) in enumerate(zip(given, operands)):
            if far_in[i]:
                arriving.append(Arriving(operand.source(ref), scratch.pop(0), in_sems.at[i]))
            else:
                arriving.append(Present(ref))
        leaving = []
        for i, ref in enumerate(results):
            if far_outs:
                leaving.append(Leaving(scratch.pop(0), ref, out_sems.at[pl.ds(i * PARTS, PARTS)]))
            else:
                leaving.append(Leaving(ref))
        body(arriving, leaving)
        for one in leaving:
            for copy in one.copies:
                copy.wait()

    here, away = pl.BlockSpec(memory_space=pltpu.VMEM), pl.BlockSpec(memory_space=pltpu.HBM)
    held = [pltpu.VMEM(o.shape, a.dtype) for o, a, is_far in zip(operands, arrays, far_in) if is_far]
    if far_outs:
        held += [pltpu.VMEM(o.shape, o.dtype) for o in outs]
    return pl.pallas_call(
        kernel,
        in_specs=[away if is_far else here for is_far in far_in],
        out_specs=[away if far_outs else here] * n_out,
        out_shape=outs,
        scratch_shapes=held
        + [pltpu.SemaphoreType.DMA((n_in,)), pltpu.SemaphoreType.DMA((n_out * PARTS,))],
        compiler_params=pltpu.CompilerParams(vmem_limit_bytes=room * 1024 * 1024),
        cost_estimate=pl.CostEstimate(flops=flops, bytes_accessed=moved, transcendentals=0),
    )(*arrays)


def as_row(block):
    return jnp.concatenate([block[i : i + 1] for i in range(block.shape[0])], axis=1)


def embed_body(arriving, leaving):
    patch, sender, geo, node, feat, in_w, out_w, edge_w, geo_w = arriving
    (box,) = leaving
    peers, box_rows, _ = box.shape
    edges = patch.held.shape[1]
    grid_rows = feat.held.shape[1]
    pieces = edge_w.held.shape[1] // LANES
    capacity = 4 * edges // (3 * peers)
    slots = peers * capacity
    me = lax.axis_index("patch")
    earlier = as_onehot(
        lax.broadcasted_iota(jnp.int32, (edges, edges), 0)
        < lax.broadcasted_iota(jnp.int32, (edges, edges), 1)
    )
    patch = patch()
    named = lax.broadcasted_iota(jnp.int32, (peers, edges), 0) == patch
    named_f = jnp.where(named, 1.0, 0.0)
    before = dot_nn(named_f.astype(BF16), earlier)
    rank = jnp.sum(named_f * before, axis=0, keepdims=True).astype(jnp.int32)
    place = rows_equal(slots, patch * capacity + rank)
    source = rows_equal(grid_rows, as_row(sender()))
    pick = dot_nt(place, source).astype(BF16)
    geo = dot_nt(place, geo()).astype(BF16)

    address = as_row(node()) + 1
    first = me * capacity
    lane = rows_equal(LANES, rank + lax.rem(first, LANES))
    high = dot_nt((named_f * (address // RADIX).astype(F32)).astype(BF16), lane)
    low = dot_nt((named_f * lax.rem(address, RADIX).astype(F32)).astype(BF16), lane)
    extra = box_rows - pieces * capacity
    row = lax.broadcasted_iota(jnp.int32, (peers, extra, LANES), 1)
    mine = first // LANES
    words = jnp.where(
        row == mine,
        high[:, None, :],
        jnp.where(row == extra // 2 + mine, low[:, None, :], 0.0),
    )
    box.held[:, pieces * capacity :, :] = words.astype(BF16)

    hidden = silu(dot_tn(feat(), in_w())).astype(BF16)
    latent = norm_rows(dot_nn(hidden, out_w())).astype(BF16)
    rows = dot_nn(pick, latent).astype(BF16)
    term = dot_nn(rows, edge_w()) + dot_nn(geo, geo_w())
    for piece in range(pieces):
        box.held[:, piece * capacity : (piece + 1) * capacity, :] = (
            term[:, piece * LANES : (piece + 1) * LANES].reshape(peers, capacity, LANES).astype(BF16)
        )
    box.send(0, peers)


def edge_shadow_body(arriving, leaving, *, count):
    edge_parts, names, edge_w = arriving[:count], arriving[count:-1], arriving[-1]
    edges_out, pre_out, ends_out, far_out, recv_out = leaving
    size = edge_parts[0].held.shape[0]
    mesh_rows = ends_out.shape[1] // 2
    far_rows = far_out.shape[1]
    for part in range(count):
        rows = slice(part * size, (part + 1) * size)
        if count == 2:
            keep = lax.axis_index("band") == part
            send = jnp.where(keep, names[0](), names[2]()[0:1])
            recv = jnp.where(keep, names[1](), names[2]()[1:2])
            edges = jnp.where(keep, edge_parts[0](), edge_parts[1]())
        else:
            send, recv, edges = names[0](), names[1](), edge_parts[0]()
        recv_out.held[:, rows] = recv
        far_out.put(rows_equal(far_rows, send - mesh_rows).T, rows.start)
        ends = [rows_equal(mesh_rows, send).T, rows_equal(mesh_rows, recv).T]
        ends_out.put(jnp.concatenate(ends, axis=1), rows.start)
        edges_out.put(edges, rows.start)
        pre_out.put(dot_nn(edges, edge_w()).astype(BF16), rows.start)
    recv_out.send(0, 1)


def bring_body(arriving, leaving):
    halo, nodes, recv_w, node_w, out_w, pair_w, sent_w = arriving
    message_out, node_pre_out, halo_out, nodes_out, pair_w_out, sent_w_out = leaving
    halo_out.put(rows_equal(nodes.held.shape[0], halo()).T)
    nodes_out.put(nodes())
    message_out.put(dot_nn(nodes(), recv_w()).astype(BF16))
    message_out.put(out_w(), nodes.held.shape[0])
    node_pre_out.put(dot_nn(nodes(), node_w()).astype(BF16))
    pair_w_out.put(pair_w())
    sent_w_out.put(sent_w())


def message_body(arriving, leaving, *, capacity):
    box, both = arriving
    (total,) = leaving
    mesh_rows, width = total.shape
    peers = box.held.shape[0]
    pieces = width // LANES
    box = box.ref()
    words = jnp.sum(box[:, pieces * capacity :, :].astype(F32), axis=0)
    half = words.shape[0] // 2
    slots = peers * capacity
    hot = []
    for group in range(slots // LANES):
        name = words[group : group + 1] * float(RADIX) + words[half + group : half + group + 1] - 1.0
        hot.append(rows_equal(mesh_rows, name.astype(jnp.int32)))
    hot = jnp.concatenate(hot, axis=1)
    terms = jnp.concatenate(
        [
            box[:, piece * capacity : (piece + 1) * capacity, :].astype(F32).reshape(slots, LANES)
            for piece in range(pieces)
        ],
        axis=1,
    )
    message = tail(terms + dot_tn(hot, both.ref()[:mesh_rows]), both.ref()[mesh_rows:]).astype(BF16)
    total.put(dot_nn(hot, message).astype(BF16))


def mesh_body(arriving, leaving, *, count):
    totals, (nodes, node_pre, pair_w, halo_hot, sent_w) = arriving[:count], arriving[count:]
    one_out, box_out = leaving
    total = totals[0]().astype(F32)
    for other in totals[1:]:
        total = total + other().astype(F32)
    preact = node_pre().astype(F32) + dot_nn(total.astype(BF16), pair_w.ref()[0])
    one = (nodes().astype(F32) + tail(preact, pair_w.ref()[1])).astype(BF16)
    one_out.put(one)
    rows = dot_nn(halo_hot(), one).astype(BF16)
    box_out.put(dot_nn(rows, sent_w()).astype(BF16))


def local_body(arriving, leaving):
    one, sent_w, recv_w, ends, pre, node_w = arriving
    pre_out, node_pre_out = leaving
    sent = dot_nn(one(), sent_w()).astype(BF16)
    recv = dot_nn(one(), recv_w()).astype(BF16)
    own = dot_nn(ends(), jnp.concatenate([sent, recv], axis=0))
    pre_out.put((pre().astype(F32) + own).astype(BF16))
    node_pre_out.put(dot_nn(one(), node_w()).astype(BF16))


def edge_values(arriving):
    far, ghosts, pre, edge_w, edges = arriving
    preact = pre().astype(F32) + dot_nn(far(), ghosts())
    return (edges().astype(F32) + tail(preact, edge_w())).astype(BF16)


def node_values(total, arriving):
    pair_w, node_pre, one = arriving
    preact = node_pre().astype(F32) + dot_nn(total, pair_w.ref()[0])
    return (one().astype(F32) + tail(preact, pair_w.ref()[1])).astype(BF16)


def edge_node_body(arriving, leaving):
    edge_out, two_out = leaving
    made = edge_values(arriving[:5])
    size = edge_out.shape[0]
    edge_out.put(jnp.where(lax.axis_index("band") == 0, made[:size], made[size:]))
    target = rows_equal(two_out.shape[0], arriving[5]())
    two_out.put(node_values(dot_nn(target, made).astype(BF16), arriving[6:]))


def edge_body(arriving, leaving):
    edge_out, total_out = leaving
    made = edge_values(arriving[:5])
    edge_out.put(made)
    total_out.put(dot_nn(rows_equal(total_out.shape[0], arriving[5]()), made).astype(BF16))


def node_body(arriving, leaving):
    leaving[0].put(node_values(arriving[0](), arriving[1:]))


def shape(dims, dtype=BF16):
    return jax.ShapeDtypeStruct(dims, dtype)


def per_device(
    grid_feat,
    enc_sender,
    enc_patch,
    enc_node,
    enc_geo,
    mesh_nodes,
    mesh_edge,
    mesh_send,
    mesh_recv,
    halo_rows,
    grid_in,
    grid_out,
    geo_weight,
    enc_edge_w,
    enc_node_w,
    proc_edge_w,
    proc_node_w,
):
    bands, peers = lax.axis_size("band"), lax.axis_size("patch")
    mesh_count, width = mesh_nodes.shape
    edge_count, medge_count = enc_sender.shape[0], mesh_edge.shape[0]
    halo_count = halo_rows.shape[1]
    capacity = 4 * edge_count // (3 * peers)
    slots = peers * capacity
    pieces = width // LANES
    address_rows = 2 * (slots // LANES)
    paired = bands == 2
    other = [(0, 1), (1, 0)]
    unit = 2 * width * width

    def band_sum(partial_value):
        share = lax.psum_scatter(partial_value, "band", scatter_dimension=0, tiled=True)
        return lax.all_gather(share, "band", axis=0, tiled=True)

    matrix, pair = shape((width, width)), shape((2, width, width))
    node_like, edge_like = shape((mesh_count, width)), shape((medge_count, width))
    sources = [
        enc_patch.reshape(1, -1),
        enc_sender.reshape(-1, LANES),
        enc_geo,
        enc_node.reshape(-1, LANES),
        grid_feat.T,
        grid_in,
        grid_out,
    ]
    (outbox,) = call(
        embed_body,
        [shape((peers, pieces * capacity + address_rows, LANES))],
        [Far(source) for source in sources] + [Far(enc_edge_w, 0), Far(geo_weight)],
        unit * 1500,
        far_outs=True,
        room=BIG,
    )
    inbox = lax.all_to_all(outbox, "patch", split_axis=0, concat_axis=0, tiled=True)

    send_row, recv_row = mesh_send.reshape(1, -1), mesh_recv.reshape(1, -1)
    edge_parts, names = [mesh_edge], [send_row, recv_row]
    if paired:
        own_edge, own_names, _ = lax.optimization_barrier(
            (mesh_edge, jnp.concatenate(names, axis=0), outbox)
        )
        edge_parts.append(lax.ppermute(own_edge, "band", other))
        names.append(lax.ppermute(own_names, "band", other))
    count = len(edge_parts)
    edge_total = count * medge_count
    nodes, _ = lax.optimization_barrier((mesh_nodes, outbox))
    message_pair, node_pre, halo_hot, nodes, node_w, sent_w = call(
        bring_body,
        [
            shape((mesh_count + width, width)),
            node_like,
            shape((halo_count, mesh_count)),
            node_like,
            pair,
            matrix,
        ],
        [
            Far(halo_rows),
            Far(nodes),
            Far(enc_edge_w, 1),
            Far(enc_node_w, 0),
            Far(enc_edge_w, 2),
            Far(enc_node_w, 1, 2),
            Far(proc_edge_w, 1),
        ],
        unit * 640,
        room=MID,
    )
    message_pair, edge_parts[-1], names[-1] = lax.optimization_barrier(
        (message_pair, edge_parts[-1], names[-1])
    )
    (partial_value,) = call(
        functools.partial(message_body, capacity=capacity),
        [node_like],
        [inbox, message_pair],
        unit * 1200,
    )
    names[0], partial_value = lax.optimization_barrier((names[0], partial_value))
    edges, edge_pre, ends, far, edge_recv = call(
        functools.partial(edge_shadow_body, count=count),
        [
            shape((edge_total, width)),
            shape((edge_total, width)),
            shape((edge_total, 2 * mesh_count)),
            shape((edge_total, halo_count)),
            shape((1, edge_total), jnp.int32),
        ],
        [Far(one) for one in edge_parts + names] + [Far(proc_edge_w, 0)],
        unit * edge_total,
        far_outs=True,
        room=MID,
    )
    if paired:
        totals = [partial_value, lax.ppermute(partial_value, "band", other)]
    else:
        totals = [band_sum(partial_value)]
    node_pre, edge_pre = lax.optimization_barrier((node_pre, edge_pre))
    mesh_one, halo_box = call(
        functools.partial(mesh_body, count=len(totals)),
        [node_like, shape((halo_count, width))],
        totals + [nodes, node_pre, node_w, halo_hot, sent_w],
        unit * 1000,
    )
    ghosts = lax.all_to_all(
        halo_box.reshape(peers, -1, width), "patch", split_axis=0, concat_axis=0, tiled=True
    ).reshape(halo_count, width)
    edge_whole = shape((edge_total, width))
    edge_pre, node_pre = call(
        local_body,
        [edge_whole, node_like],
        [mesh_one, sent_w, Far(proc_edge_w, 2), Far(ends), Far(edge_pre), Far(proc_node_w, 0)],
        unit * 1500,
        far_outs=True,
        room=MID,
    )
    edge_operands = [Far(far), Far(ghosts), Far(edge_pre), Far(proc_edge_w, 3), Far(edges), Far(edge_recv)]
    node_operands = [Far(proc_node_w, 1, 2), Far(node_pre), Far(mesh_one)]
    if paired:
        edge_out, mesh_two = call(
            edge_node_body,
            [edge_like, node_like],
            edge_operands + node_operands,
            unit * 1500,
            far_outs=True,
            room=BIG,
        )
    else:
        edge_out, partial_two = call(
            edge_body, [edge_like, node_like], edge_operands, unit * 800, far_outs=True, room=BIG
        )
        (mesh_two,) = call(
            node_body,
            [node_like],
            [Far(band_sum(partial_two))] + node_operands,
            unit * 640,
            far_outs=True,
            room=BIG,
        )
    return (mesh_two, edge_out)


def solution(mesh):
    both = ("band", "patch")
    in_specs = (
        P(both, None),
        P(both),
        P(both, None),
        P(both),
        P(None, both),
        P("patch", None),
        P(both, None),
        P(both),
        P(both),
        P("patch", None),
        P(),
        P(),
        P(),
        P(),
        P(),
        P(),
        P(),
    )
    out_specs = (P("patch", None), P(both, None))
    return jax.shard_map(
        per_device, mesh=mesh, in_specs=in_specs, out_specs=out_specs, check_vma=False
    )
```

```python
import functools
import math

import jax
import jax.numpy as jnp
from jax import lax
from jax.experimental import pallas as pl
from jax.experimental.pallas import tpu as pltpu
from jax.sharding import PartitionSpec as P

F32 = jnp.float32
BF16 = jnp.bfloat16
LANES = 128
RADIX = 32


def dot_nn(left, right):
    return jnp.dot(left, right, preferred_element_type=F32)


def dot_nt(left, right):
    return lax.dot_general(left, right, (((1,), (1,)), ((), ())), preferred_element_type=F32)


def dot_tn(left, right):
    return lax.dot_general(left, right, (((0,), (0,)), ((), ())), preferred_element_type=F32)


def as_onehot(hits):
    return jnp.where(hits, 1.0, 0.0).astype(BF16)


def rows_equal(row_count, names):
    rows = lax.broadcasted_iota(jnp.int32, (row_count, names.shape[1]), 0)
    return as_onehot(rows == names)


def norm_rows(values_in):
    average = jnp.mean(values_in, axis=-1, keepdims=True)
    centred = values_in - average
    spread = jnp.mean(centred * centred, axis=-1, keepdims=True)
    return centred * lax.rsqrt(spread + 1e-05)


def silu(values_in):
    return values_in * jax.nn.sigmoid(values_in)


def tail(preact, out_weight):
    return norm_rows(dot_nn(silu(preact).astype(BF16), out_weight))


class Arriving:
    def __init__(self, source, held, sem):
        self.held, self.copy, self.waited = held, pltpu.make_async_copy(source, held, sem), False
        self.copy.start()

    def ref(self):
        if not self.waited:
            self.copy.wait()
            self.waited = True
        return self.held

    def __call__(self):
        return self.ref()[...]


class Present:
    def __init__(self, held):
        self.held = held

    def ref(self):
        return self.held

    def __call__(self):
        return self.held[...]


class Leaving:
    def __init__(self, held, target=None, sems=None):
        self.held, self.target, self.sems, self.copies = held, target, sems, []
        self.shape = held.shape

    def send(self, first, count):
        if self.target is not None:
            rows = pl.ds(first, count)
            copy = pltpu.make_async_copy(
                self.held.at[rows], self.target.at[rows], self.sems.at[len(self.copies)]
            )
            copy.start()
            self.copies.append(copy)

    def put(self, value, first=0):
        self.held[first : first + value.shape[0]] = value
        self.send(first, value.shape[0])


class Far:
    def __init__(self, array, index=None, count=None):
        self.array, self.index, self.count = array, index, count
        self.shape = array.shape
        if index is not None:
            self.shape = array.shape[1:] if count is None else (count,) + array.shape[1:]

    def source(self, ref):
        if self.index is None:
            return ref
        return ref.at[self.index if self.count is None else pl.ds(self.index, self.count)]


PARTS = 4
BIG, ROOM = 60, 48


def call(body, outs, operands, flops, far_outs=False, room=ROOM):
    n_in, n_out = len(operands), len(outs)
    far_in = [isinstance(operand, Far) for operand in operands]
    arrays = [operand.array if away else operand for operand, away in zip(operands, far_in)]
    moved = sum(math.prod(o.shape) * a.dtype.itemsize for o, a in zip(operands, arrays))

    def kernel(*refs):
        given, results, scratch = refs[:n_in], refs[n_in : n_in + n_out], list(refs[n_in + n_out : -2])
        in_sems, out_sems = refs[-2:]
        arriving = []
        for i, (ref, operand) in enumerate(zip(given, operands)):
            if far_in[i]:
                arriving.append(Arriving(operand.source(ref), scratch.pop(0), in_sems.at[i]))
            else:
                arriving.append(Present(ref))
        leaving = []
        for i, ref in enumerate(results):
            if far_outs:
                leaving.append(Leaving(scratch.pop(0), ref, out_sems.at[pl.ds(i * PARTS, PARTS)]))
            else:
                leaving.append(Leaving(ref))
        body(arriving, leaving)
        for one in leaving:
            for copy in one.copies:
                copy.wait()

    here, away = pl.BlockSpec(memory_space=pltpu.VMEM), pl.BlockSpec(memory_space=pltpu.HBM)
    held = [pltpu.VMEM(o.shape, a.dtype) for o, a, is_far in zip(operands, arrays, far_in) if is_far]
    if far_outs:
        held += [pltpu.VMEM(o.shape, o.dtype) for o in outs]
    return pl.pallas_call(
        kernel,
        in_specs=[away if is_far else here for is_far in far_in],
        out_specs=[away if far_outs else here] * n_out,
        out_shape=outs,
        scratch_shapes=held
        + [pltpu.SemaphoreType.DMA((n_in,)), pltpu.SemaphoreType.DMA((n_out * PARTS,))],
        compiler_params=pltpu.CompilerParams(vmem_limit_bytes=room * 1024 * 1024),
        cost_estimate=pl.CostEstimate(flops=flops, bytes_accessed=moved, transcendentals=0),
    )(*arrays)


def as_row(block):
    return jnp.concatenate([block[i : i + 1] for i in range(block.shape[0])], axis=1)


def embed_body(arriving, leaving):
    patch, sender, geo, node, feat, in_w, out_w, edge_w, geo_w = arriving
    (box,) = leaving
    peers, box_rows, _ = box.shape
    edges = patch.held.shape[1]
    grid_rows = feat.held.shape[1]
    pieces = edge_w.held.shape[1] // LANES
    capacity = 4 * edges // (3 * peers)
    slots = peers * capacity
    me = lax.axis_index("patch")
    earlier = as_onehot(
        lax.broadcasted_iota(jnp.int32, (edges, edges), 0)
        < lax.broadcasted_iota(jnp.int32, (edges, edges), 1)
    )
    for one in arriving:
        one.ref()
    patch = patch()
    named = lax.broadcasted_iota(jnp.int32, (peers, edges), 0) == patch
    named_f = jnp.where(named, 1.0, 0.0)
    before = dot_nn(named_f.astype(BF16), earlier)
    rank = jnp.sum(named_f * before, axis=0, keepdims=True).astype(jnp.int32)
    place = rows_equal(slots, patch * capacity + rank)
    source = rows_equal(grid_rows, as_row(sender()))
    pick = dot_nt(place, source).astype(BF16)
    geo = dot_nt(place, geo()).astype(BF16)

    address = as_row(node()) + 1
    first = me * capacity
    lane = rows_equal(LANES, rank + lax.rem(first, LANES))
    high = dot_nt((named_f * (address // RADIX).astype(F32)).astype(BF16), lane)
    low = dot_nt((named_f * lax.rem(address, RADIX).astype(F32)).astype(BF16), lane)
    extra = box_rows - pieces * capacity
    row = lax.broadcasted_iota(jnp.int32, (peers, extra, LANES), 1)
    mine = first // LANES
    words = jnp.where(
        row == mine,
        high[:, None, :],
        jnp.where(row == extra // 2 + mine, low[:, None, :], 0.0),
    )
    box.held[:, pieces * capacity :, :] = words.astype(BF16)

    hidden = silu(dot_tn(feat(), in_w())).astype(BF16)
    latent = norm_rows(dot_nn(hidden, out_w())).astype(BF16)
    rows = dot_nn(pick, latent).astype(BF16)
    term = dot_nn(rows, edge_w()) + dot_nn(geo, geo_w())
    for piece in range(pieces):
        box.held[:, piece * capacity : (piece + 1) * capacity, :] = (
            term[:, piece * LANES : (piece + 1) * LANES].reshape(peers, capacity, LANES).astype(BF16)
        )
    box.send(0, peers)


def edge_shadow_body(arriving, leaving, *, count):
    edge_parts, names, edge_w = arriving[:count], arriving[count:-1], arriving[-1]
    edges_out, pre_out, ends_out, far_out, recv_out = leaving
    size = edge_parts[0].held.shape[0]
    mesh_rows = ends_out.shape[1] // 2
    far_rows = far_out.shape[1]
    for part in range(count):
        rows = slice(part * size, (part + 1) * size)
        if count == 2:
            keep = lax.axis_index("band") == part
            send = jnp.where(keep, names[0](), names[2]()[0:1])
            recv = jnp.where(keep, names[1](), names[2]()[1:2])
            edges = jnp.where(keep, edge_parts[0](), edge_parts[1]())
        else:
            send, recv, edges = names[0](), names[1](), edge_parts[0]()
        recv_out.held[:, rows] = recv
        far_out.put(rows_equal(far_rows, send - mesh_rows).T, rows.start)
        ends = [rows_equal(mesh_rows, send).T, rows_equal(mesh_rows, recv).T]
        ends_out.put(jnp.concatenate(ends, axis=1), rows.start)
        edges_out.put(edges, rows.start)
        pre_out.put(dot_nn(edges, edge_w()).astype(BF16), rows.start)
    recv_out.send(0, 1)


def message_bring_body(arriving, leaving):
    nodes, recv_w, out_w = arriving
    (both,) = leaving
    both.put(dot_nn(nodes(), recv_w()).astype(BF16))
    both.put(out_w(), nodes.held.shape[0])


def mesh_bring_body(arriving, leaving):
    halo, nodes, node_w, pair_w, sent_w = arriving
    node_pre_out, halo_out, nodes_out, pair_w_out, sent_w_out = leaving
    halo_out.put(rows_equal(nodes.held.shape[0], halo()).T)
    nodes_out.put(nodes())
    node_pre_out.put(dot_nn(nodes(), node_w()).astype(BF16))
    pair_w_out.put(pair_w())
    sent_w_out.put(sent_w())


def message_body(arriving, leaving, *, capacity):
    box, both = arriving
    (total,) = leaving
    mesh_rows, width = total.shape
    peers = box.held.shape[0]
    pieces = width // LANES
    box = box.ref()
    words = jnp.sum(box[:, pieces * capacity :, :].astype(F32), axis=0)
    half = words.shape[0] // 2
    slots = peers * capacity
    hot = []
    for group in range(slots // LANES):
        name = words[group : group + 1] * float(RADIX) + words[half + group : half + group + 1] - 1.0
        hot.append(rows_equal(mesh_rows, name.astype(jnp.int32)))
    hot = jnp.concatenate(hot, axis=1)
    terms = jnp.concatenate(
        [
            box[:, piece * capacity : (piece + 1) * capacity, :].astype(F32).reshape(slots, LANES)
            for piece in range(pieces)
        ],
        axis=1,
    )
    message = tail(terms + dot_tn(hot, both.ref()[:mesh_rows]), both.ref()[mesh_rows:]).astype(BF16)
    total.put(dot_nn(hot, message).astype(BF16))


def mesh_body(arriving, leaving, *, count):
    totals, (nodes, node_pre, pair_w, halo_hot, sent_w) = arriving[:count], arriving[count:]
    one_out, box_out = leaving
    total = totals[0]().astype(F32)
    for other in totals[1:]:
        total = total + other().astype(F32)
    preact = node_pre().astype(F32) + dot_nn(total.astype(BF16), pair_w.ref()[0])
    one = (nodes().astype(F32) + tail(preact, pair_w.ref()[1])).astype(BF16)
    one_out.put(one)
    rows = dot_nn(halo_hot(), one).astype(BF16)
    box_out.put(dot_nn(rows, sent_w()).astype(BF16))


def local_body(arriving, leaving):
    one, sent_w, recv_w, ends, pre, node_w = arriving
    pre_out, node_pre_out = leaving
    sent = dot_nn(one(), sent_w()).astype(BF16)
    recv = dot_nn(one(), recv_w()).astype(BF16)
    own = dot_nn(ends(), jnp.concatenate([sent, recv], axis=0))
    pre_out.put((pre().astype(F32) + own).astype(BF16))
    node_pre_out.put(dot_nn(one(), node_w()).astype(BF16))


def edge_values(arriving):
    far, ghosts, pre, edge_w, edges = arriving
    preact = pre().astype(F32) + dot_nn(far(), ghosts())
    return (edges().astype(F32) + tail(preact, edge_w())).astype(BF16)


def node_values(total, arriving):
    pair_w, node_pre, one = arriving
    preact = node_pre().astype(F32) + dot_nn(total, pair_w.ref()[0])
    return (one().astype(F32) + tail(preact, pair_w.ref()[1])).astype(BF16)


def edge_node_body(arriving, leaving):
    edge_out, two_out = leaving
    made = edge_values(arriving[:5])
    size = edge_out.shape[0]
    edge_out.put(jnp.where(lax.axis_index("band") == 0, made[:size], made[size:]))
    target = rows_equal(two_out.shape[0], arriving[5]())
    two_out.put(node_values(dot_nn(target, made).astype(BF16), arriving[6:]))


def edge_body(arriving, leaving):
    edge_out, total_out = leaving
    made = edge_values(arriving[:5])
    edge_out.put(made)
    total_out.put(dot_nn(rows_equal(total_out.shape[0], arriving[5]()), made).astype(BF16))


def node_body(arriving, leaving):
    leaving[0].put(node_values(arriving[0](), arriving[1:]))


def shape(dims, dtype=BF16):
    return jax.ShapeDtypeStruct(dims, dtype)


def per_device(
    grid_feat,
    enc_sender,
    enc_patch,
    enc_node,
    enc_geo,
    mesh_nodes,
    mesh_edge,
    mesh_send,
    mesh_recv,
    halo_rows,
    grid_in,
    grid_out,
    geo_weight,
    enc_edge_w,
    enc_node_w,
    proc_edge_w,
    proc_node_w,
):
    bands, peers = lax.axis_size("band"), lax.axis_size("patch")
    mesh_count, width = mesh_nodes.shape
    edge_count, medge_count = enc_sender.shape[0], mesh_edge.shape[0]
    halo_count = halo_rows.shape[1]
    capacity = 4 * edge_count // (3 * peers)
    slots = peers * capacity
    pieces = width // LANES
    address_rows = 2 * (slots // LANES)
    paired = bands == 2
    other = [(0, 1), (1, 0)]
    unit = 2 * width * width

    def band_sum(partial_value):
        share = lax.psum_scatter(partial_value, "band", scatter_dimension=0, tiled=True)
        return lax.all_gather(share, "band", axis=0, tiled=True)

    matrix, pair = shape((width, width)), shape((2, width, width))
    node_like, edge_like = shape((mesh_count, width)), shape((medge_count, width))
    sources = [
        enc_patch.reshape(1, -1),
        enc_sender.reshape(-1, LANES),
        enc_geo,
        enc_node.reshape(-1, LANES),
        grid_feat.T,
        grid_in,
        grid_out,
    ]
    (outbox,) = call(
        embed_body,
        [shape((peers, pieces * capacity + address_rows, LANES))],
        [Far(source) for source in sources] + [Far(enc_edge_w, 0), Far(geo_weight)],
        unit * 1500,
        far_outs=True,
        room=BIG,
    )
    inbox = lax.all_to_all(outbox, "patch", split_axis=0, concat_axis=0, tiled=True)

    send_row, recv_row = mesh_send.reshape(1, -1), mesh_recv.reshape(1, -1)
    edge_parts, names = [mesh_edge], [send_row, recv_row]
    if paired:
        own_edge, own_names, _ = lax.optimization_barrier(
            (mesh_edge, jnp.concatenate(names, axis=0), outbox)
        )
        edge_parts.append(lax.ppermute(own_edge, "band", other))
        names.append(lax.ppermute(own_names, "band", other))
    count = len(edge_parts)
    edge_total = count * medge_count
    nodes, _ = lax.optimization_barrier((mesh_nodes, outbox))
    (message_pair,) = call(
        message_bring_body,
        [shape((mesh_count + width, width))],
        [Far(nodes), Far(enc_edge_w, 1), Far(enc_edge_w, 2)],
        unit * 320,
        room=ROOM,
    )
    message_pair, edge_parts[-1], names[-1] = lax.optimization_barrier(
        (message_pair, edge_parts[-1], names[-1])
    )
    (partial_value,) = call(
        functools.partial(message_body, capacity=capacity),
        [node_like],
        [inbox, message_pair],
        unit * 1200,
    )
    names[0], partial_value = lax.optimization_barrier((names[0], partial_value))
    edges, edge_pre, ends, far, edge_recv = call(
        functools.partial(edge_shadow_body, count=count),
        [
            shape((edge_total, width)),
            shape((edge_total, width)),
            shape((edge_total, 2 * mesh_count)),
            shape((edge_total, halo_count)),
            shape((1, edge_total), jnp.int32),
        ],
        [Far(one) for one in edge_parts + names] + [Far(proc_edge_w, 0)],
        unit * edge_total,
        far_outs=True,
        room=ROOM,
    )
    if paired:
        totals = [partial_value, lax.ppermute(partial_value, "band", other)]
    else:
        totals = [band_sum(partial_value)]
    nodes, halo_rows, _ = lax.optimization_barrier((mesh_nodes, halo_rows, partial_value))
    node_pre, halo_hot, nodes, node_w, sent_w = call(
        mesh_bring_body,
        [node_like, shape((halo_count, mesh_count)), node_like, pair, matrix],
        [Far(halo_rows), Far(nodes), Far(enc_node_w, 0), Far(enc_node_w, 1, 2), Far(proc_edge_w, 1)],
        unit * 320,
        room=ROOM,
    )
    node_pre, edge_pre = lax.optimization_barrier((node_pre, edge_pre))
    mesh_one, halo_box = call(
        functools.partial(mesh_body, count=len(totals)),
        [node_like, shape((halo_count, width))],
        totals + [nodes, node_pre, node_w, halo_hot, sent_w],
        unit * 1000,
    )
    ghosts = lax.all_to_all(
        halo_box.reshape(peers, -1, width), "patch", split_axis=0, concat_axis=0, tiled=True
    ).reshape(halo_count, width)
    edge_whole = shape((edge_total, width))
    edge_pre, node_pre = call(
        local_body,
        [edge_whole, node_like],
        [mesh_one, sent_w, Far(proc_edge_w, 2), Far(ends), Far(edge_pre), Far(proc_node_w, 0)],
        unit * 1500,
        far_outs=True,
        room=ROOM,
    )
    edge_operands = [Far(far), Far(ghosts), Far(edge_pre), Far(proc_edge_w, 3), Far(edges), Far(edge_recv)]
    node_operands = [Far(proc_node_w, 1, 2), Far(node_pre), Far(mesh_one)]
    if paired:
        edge_out, mesh_two = call(
            edge_node_body,
            [edge_like, node_like],
            edge_operands + node_operands,
            unit * 1500,
            far_outs=True,
            room=BIG,
        )
    else:
        edge_out, partial_two = call(
            edge_body, [edge_like, node_like], edge_operands, unit * 800, far_outs=True, room=BIG
        )
        (mesh_two,) = call(
            node_body,
            [node_like],
            [Far(band_sum(partial_two))] + node_operands,
            unit * 640,
            far_outs=True,
            room=BIG,
        )
    return (mesh_two, edge_out)


def solution(mesh):
    both = ("band", "patch")
    in_specs = (
        P(both, None),
        P(both),
        P(both, None),
        P(both),
        P(None, both),
        P("patch", None),
        P(both, None),
        P(both),
        P(both),
        P("patch", None),
        P(),
        P(),
        P(),
        P(),
        P(),
        P(),
        P(),
    )
    out_specs = (P("patch", None), P(both, None))
    return jax.shard_map(
        per_device, mesh=mesh, in_specs=in_specs, out_specs=out_specs, check_vma=False
    )
```

```python
import functools
import math

import jax
import jax.numpy as jnp
from jax import lax
from jax.experimental import pallas as pl
from jax.experimental.pallas import tpu as pltpu
from jax.sharding import PartitionSpec as P

F32 = jnp.float32
BF16 = jnp.bfloat16
LANES = 128
RADIX = 32


def dot_nn(left, right):
    return jnp.dot(left, right, preferred_element_type=F32)


def dot_nt(left, right):
    return lax.dot_general(left, right, (((1,), (1,)), ((), ())), preferred_element_type=F32)


def dot_tn(left, right):
    return lax.dot_general(left, right, (((0,), (0,)), ((), ())), preferred_element_type=F32)


def as_onehot(hits):
    return jnp.where(hits, 1.0, 0.0).astype(BF16)


def rows_equal(row_count, names):
    rows = lax.broadcasted_iota(jnp.int32, (row_count, names.shape[1]), 0)
    return as_onehot(rows == names)


def norm_rows(values_in):
    average = jnp.mean(values_in, axis=-1, keepdims=True)
    centred = values_in - average
    spread = jnp.mean(centred * centred, axis=-1, keepdims=True)
    return centred * lax.rsqrt(spread + 1e-05)


def silu(values_in):
    return values_in * jax.nn.sigmoid(values_in)


def tail(preact, out_weight):
    return norm_rows(dot_nn(silu(preact).astype(BF16), out_weight))


class Arriving:
    def __init__(self, source, held, sem):
        self.held, self.copy, self.waited = held, pltpu.make_async_copy(source, held, sem), False
        self.copy.start()

    def ref(self):
        if not self.waited:
            self.copy.wait()
            self.waited = True
        return self.held

    def __call__(self):
        return self.ref()[...]


class Present:
    def __init__(self, held):
        self.held = held

    def ref(self):
        return self.held

    def __call__(self):
        return self.held[...]


class Leaving:
    def __init__(self, held, target=None, sems=None):
        self.held, self.target, self.sems, self.copies = held, target, sems, []
        self.shape = held.shape

    def send(self, first, count):
        if self.target is not None:
            rows = pl.ds(first, count)
            copy = pltpu.make_async_copy(
                self.held.at[rows], self.target.at[rows], self.sems.at[len(self.copies)]
            )
            copy.start()
            self.copies.append(copy)

    def put(self, value, first=0):
        self.held[first : first + value.shape[0]] = value
        self.send(first, value.shape[0])


class Far:
    def __init__(self, array, index=None, count=None):
        self.array, self.index, self.count = array, index, count
        self.shape = array.shape
        if index is not None:
            self.shape = array.shape[1:] if count is None else (count,) + array.shape[1:]

    def source(self, ref):
        if self.index is None:
            return ref
        return ref.at[self.index if self.count is None else pl.ds(self.index, self.count)]


PARTS = 4
BIG, ROOM = 60, 48


def call(body, outs, operands, flops, far_outs=False, room=ROOM):
    n_in, n_out = len(operands), len(outs)
    far_in = [isinstance(operand, Far) for operand in operands]
    arrays = [operand.array if away else operand for operand, away in zip(operands, far_in)]
    moved = sum(math.prod(o.shape) * a.dtype.itemsize for o, a in zip(operands, arrays))

    def kernel(*refs):
        given, results, scratch = refs[:n_in], refs[n_in : n_in + n_out], list(refs[n_in + n_out : -2])
        in_sems, out_sems = refs[-2:]
        arriving = []
        for i, (ref, operand) in enumerate(zip(given, operands)):
            if far_in[i]:
                arriving.append(Arriving(operand.source(ref), scratch.pop(0), in_sems.at[i]))
            else:
                arriving.append(Present(ref))
        leaving = []
        for i, ref in enumerate(results):
            if far_outs:
                leaving.append(Leaving(scratch.pop(0), ref, out_sems.at[pl.ds(i * PARTS, PARTS)]))
            else:
                leaving.append(Leaving(ref))
        body(arriving, leaving)
        for one in leaving:
            for copy in one.copies:
                copy.wait()

    here, away = pl.BlockSpec(memory_space=pltpu.VMEM), pl.BlockSpec(memory_space=pltpu.HBM)
    held = [pltpu.VMEM(o.shape, a.dtype) for o, a, is_far in zip(operands, arrays, far_in) if is_far]
    if far_outs:
        held += [pltpu.VMEM(o.shape, o.dtype) for o in outs]
    return pl.pallas_call(
        kernel,
        in_specs=[away if is_far else here for is_far in far_in],
        out_specs=[away if far_outs else here] * n_out,
        out_shape=outs,
        scratch_shapes=held
        + [pltpu.SemaphoreType.DMA((n_in,)), pltpu.SemaphoreType.DMA((n_out * PARTS,))],
        compiler_params=pltpu.CompilerParams(vmem_limit_bytes=int(room * 1024) * 1024),
        cost_estimate=pl.CostEstimate(flops=flops, bytes_accessed=moved, transcendentals=0),
    )(*arrays)


def as_row(block):
    return jnp.concatenate([block[i : i + 1] for i in range(block.shape[0])], axis=1)


def embed_body(arriving, leaving):
    patch, sender, geo, node, feat, in_w, out_w, edge_w, geo_w = arriving
    (box,) = leaving
    peers, box_rows, _ = box.shape
    edges = patch.held.shape[1]
    grid_rows = feat.held.shape[1]
    pieces = edge_w.held.shape[1] // LANES
    capacity = 4 * edges // (3 * peers)
    slots = peers * capacity
    me = lax.axis_index("patch")
    earlier = as_onehot(
        lax.broadcasted_iota(jnp.int32, (edges, edges), 0)
        < lax.broadcasted_iota(jnp.int32, (edges, edges), 1)
    )
    patch = patch()
    named = lax.broadcasted_iota(jnp.int32, (peers, edges), 0) == patch
    named_f = jnp.where(named, 1.0, 0.0)
    before = dot_nn(named_f.astype(BF16), earlier)
    rank = jnp.sum(named_f * before, axis=0, keepdims=True).astype(jnp.int32)
    for one in arriving:
        one.ref()
    place = rows_equal(slots, patch * capacity + rank)
    source = rows_equal(grid_rows, as_row(sender()))
    pick = dot_nt(place, source).astype(BF16)
    geo = dot_nt(place, geo()).astype(BF16)

    address = as_row(node()) + 1
    first = me * capacity
    lane = rows_equal(LANES, rank + lax.rem(first, LANES))
    high = dot_nt((named_f * (address // RADIX).astype(F32)).astype(BF16), lane)
    low = dot_nt((named_f * lax.rem(address, RADIX).astype(F32)).astype(BF16), lane)
    extra = box_rows - pieces * capacity
    row = lax.broadcasted_iota(jnp.int32, (peers, extra, LANES), 1)
    mine = first // LANES
    words = jnp.where(
        row == mine,
        high[:, None, :],
        jnp.where(row == extra // 2 + mine, low[:, None, :], 0.0),
    )
    box.held[:, pieces * capacity :, :] = words.astype(BF16)

    hidden = silu(dot_tn(feat(), in_w())).astype(BF16)
    latent = norm_rows(dot_nn(hidden, out_w())).astype(BF16)
    rows = dot_nn(pick, latent).astype(BF16)
    some = peers // PARTS
    for part in range(PARTS):
        own = slice(part * some * capacity, (part + 1) * some * capacity)
        term = dot_nn(rows[own], edge_w()) + dot_nn(geo[own], geo_w())
        for piece in range(pieces):
            box.held[part * some : (part + 1) * some, piece * capacity : (piece + 1) * capacity, :] = (
                term[:, piece * LANES : (piece + 1) * LANES].reshape(some, capacity, LANES).astype(BF16)
            )
        box.send(part * some, some)


def edge_shadow_body(arriving, leaving, *, count):
    edge_parts, names, edge_w = arriving[:count], arriving[count:-1], arriving[-1]
    edges_out, pre_out, ends_out, far_out, recv_out = leaving
    size = edge_parts[0].held.shape[0]
    mesh_rows = ends_out.shape[1] // 2
    far_rows = far_out.shape[1]
    for part in range(count):
        rows = slice(part * size, (part + 1) * size)
        if count == 2:
            keep = lax.axis_index("band") == part
            send = jnp.where(keep, names[0](), names[2]()[0:1])
            recv = jnp.where(keep, names[1](), names[2]()[1:2])
            edges = jnp.where(keep, edge_parts[0](), edge_parts[1]())
        else:
            send, recv, edges = names[0](), names[1](), edge_parts[0]()
        recv_out.held[:, rows] = recv
        far_out.put(rows_equal(far_rows, send - mesh_rows).T, rows.start)
        ends = [rows_equal(mesh_rows, send).T, rows_equal(mesh_rows, recv).T]
        ends_out.put(jnp.concatenate(ends, axis=1), rows.start)
        edges_out.put(edges, rows.start)
        pre_out.put(dot_nn(edges, edge_w()).astype(BF16), rows.start)
    recv_out.send(0, 1)


def message_bring_body(arriving, leaving):
    nodes, recv_w, out_w = arriving
    (both,) = leaving
    both.put(dot_nn(nodes(), recv_w()).astype(BF16))
    both.put(out_w(), nodes.held.shape[0])


def mesh_bring_body(arriving, leaving):
    halo, nodes, node_w, pair_w, sent_w = arriving
    node_pre_out, halo_out, nodes_out, pair_w_out, sent_w_out = leaving
    halo_out.put(rows_equal(nodes.held.shape[0], halo()).T)
    nodes_out.put(nodes())
    node_pre_out.put(dot_nn(nodes(), node_w()).astype(BF16))
    pair_w_out.put(pair_w())
    sent_w_out.put(sent_w())


def message_body(arriving, leaving, *, capacity):
    box, both = arriving
    (total,) = leaving
    mesh_rows, width = total.shape
    peers = box.held.shape[0]
    pieces = width // LANES
    box = box.ref()
    words = jnp.sum(box[:, pieces * capacity :, :].astype(F32), axis=0)
    half = words.shape[0] // 2
    slots = peers * capacity
    hot = []
    for group in range(slots // LANES):
        name = words[group : group + 1] * float(RADIX) + words[half + group : half + group + 1] - 1.0
        hot.append(rows_equal(mesh_rows, name.astype(jnp.int32)))
    hot = jnp.concatenate(hot, axis=1)
    terms = jnp.concatenate(
        [
            box[:, piece * capacity : (piece + 1) * capacity, :].astype(F32).reshape(slots, LANES)
            for piece in range(pieces)
        ],
        axis=1,
    )
    message = tail(terms + dot_tn(hot, both.ref()[:mesh_rows]), both.ref()[mesh_rows:]).astype(BF16)
    total.put(dot_nn(hot, message).astype(BF16))


def mesh_body(arriving, leaving, *, count):
    totals, (nodes, node_pre, pair_w, halo_hot, sent_w) = arriving[:count], arriving[count:]
    one_out, box_out = leaving
    total = totals[0]().astype(F32)
    for other in totals[1:]:
        total = total + other().astype(F32)
    preact = node_pre().astype(F32) + dot_nn(total.astype(BF16), pair_w.ref()[0])
    one = (nodes().astype(F32) + tail(preact, pair_w.ref()[1])).astype(BF16)
    one_out.put(one)
    rows = dot_nn(halo_hot(), one).astype(BF16)
    box_out.put(dot_nn(rows, sent_w()).astype(BF16))


def local_body(arriving, leaving):
    one, sent_w, recv_w, ends, pre, node_w = arriving
    pre_out, node_pre_out = leaving
    sent = dot_nn(one(), sent_w()).astype(BF16)
    recv = dot_nn(one(), recv_w()).astype(BF16)
    own = dot_nn(ends(), jnp.concatenate([sent, recv], axis=0))
    pre_out.put((pre().astype(F32) + own).astype(BF16))
    node_pre_out.put(dot_nn(one(), node_w()).astype(BF16))


def edge_values(arriving):
    far, ghosts, pre, edge_w, edges = arriving
    preact = dot_nn(far(), ghosts()) + pre().astype(F32)
    return (edges().astype(F32) + tail(preact, edge_w())).astype(BF16)


def node_values(total, arriving):
    pair_w, node_pre, one = arriving
    preact = node_pre().astype(F32) + dot_nn(total, pair_w.ref()[0])
    return (one().astype(F32) + tail(preact, pair_w.ref()[1])).astype(BF16)


def edge_node_body(arriving, leaving):
    edge_out, two_out = leaving
    made = edge_values(arriving[:5])
    size = edge_out.shape[0]
    edge_out.put(jnp.where(lax.axis_index("band") == 0, made[:size], made[size:]))
    target = rows_equal(two_out.shape[0], arriving[5]())
    two_out.put(node_values(dot_nn(target, made).astype(BF16), arriving[6:]))


def edge_body(arriving, leaving):
    edge_out, total_out = leaving
    made = edge_values(arriving[:5])
    edge_out.put(made)
    total_out.put(dot_nn(rows_equal(total_out.shape[0], arriving[5]()), made).astype(BF16))


def node_body(arriving, leaving):
    leaving[0].put(node_values(arriving[0](), arriving[1:]))


def shape(dims, dtype=BF16):
    return jax.ShapeDtypeStruct(dims, dtype)


def per_device(
    grid_feat,
    enc_sender,
    enc_patch,
    enc_node,
    enc_geo,
    mesh_nodes,
    mesh_edge,
    mesh_send,
    mesh_recv,
    halo_rows,
    grid_in,
    grid_out,
    geo_weight,
    enc_edge_w,
    enc_node_w,
    proc_edge_w,
    proc_node_w,
):
    bands, peers = lax.axis_size("band"), lax.axis_size("patch")
    mesh_count, width = mesh_nodes.shape
    edge_count, medge_count = enc_sender.shape[0], mesh_edge.shape[0]
    halo_count = halo_rows.shape[1]
    capacity = 4 * edge_count // (3 * peers)
    slots = peers * capacity
    pieces = width // LANES
    address_rows = 2 * (slots // LANES)
    paired = bands == 2
    other = [(0, 1), (1, 0)]
    unit = 2 * width * width

    def band_sum(partial_value):
        share = lax.psum_scatter(partial_value, "band", scatter_dimension=0, tiled=True)
        return lax.all_gather(share, "band", axis=0, tiled=True)

    matrix, pair = shape((width, width)), shape((2, width, width))
    node_like, edge_like = shape((mesh_count, width)), shape((medge_count, width))
    sources = [
        enc_patch.reshape(1, -1),
        enc_sender.reshape(-1, LANES),
        enc_geo,
        enc_node.reshape(-1, LANES),
        grid_feat.T,
        grid_in,
        grid_out,
    ]
    (outbox,) = call(
        embed_body,
        [shape((peers, pieces * capacity + address_rows, LANES))],
        [Far(source) for source in sources] + [Far(enc_edge_w, 0), Far(geo_weight)],
        unit * 1500,
        far_outs=True,
        room=BIG,
    )
    inbox = lax.all_to_all(outbox, "patch", split_axis=0, concat_axis=0, tiled=True)

    send_row, recv_row = mesh_send.reshape(1, -1), mesh_recv.reshape(1, -1)
    edge_parts, names = [mesh_edge], [send_row, recv_row]
    if paired:
        own_edge, own_names, _ = lax.optimization_barrier(
            (mesh_edge, jnp.concatenate(names, axis=0), outbox)
        )
        edge_parts.append(lax.ppermute(own_edge, "band", other))
        names.append(lax.ppermute(own_names, "band", other))
    count = len(edge_parts)
    edge_total = count * medge_count
    nodes, _ = lax.optimization_barrier((mesh_nodes, outbox))
    (message_pair,) = call(
        message_bring_body,
        [shape((mesh_count + width, width))],
        [Far(nodes), Far(enc_edge_w, 1), Far(enc_edge_w, 2)],
        unit * 320,
        room=ROOM,
    )
    message_pair, edge_parts[-1], names[-1] = lax.optimization_barrier(
        (message_pair, edge_parts[-1], names[-1])
    )
    (partial_value,) = call(
        functools.partial(message_body, capacity=capacity),
        [node_like],
        [inbox, message_pair],
        unit * 1200,
    )
    names[0], partial_value = lax.optimization_barrier((names[0], partial_value))
    edges, edge_pre, ends, far, edge_recv = call(
        functools.partial(edge_shadow_body, count=count),
        [
            shape((edge_total, width)),
            shape((edge_total, width)),
            shape((edge_total, 2 * mesh_count)),
            shape((edge_total, halo_count)),
            shape((1, edge_total), jnp.int32),
        ],
        [Far(one) for one in edge_parts + names] + [Far(proc_edge_w, 0)],
        unit * edge_total,
        far_outs=True,
        room=ROOM,
    )
    if paired:
        totals = [partial_value, lax.ppermute(partial_value, "band", other)]
    else:
        totals = [band_sum(partial_value)]
    nodes, halo_rows, _ = lax.optimization_barrier((mesh_nodes, halo_rows, partial_value))
    node_pre, halo_hot, nodes, node_w, sent_w = call(
        mesh_bring_body,
        [node_like, shape((halo_count, mesh_count)), node_like, pair, matrix],
        [Far(halo_rows), Far(nodes), Far(enc_node_w, 0), Far(enc_node_w, 1, 2), Far(proc_edge_w, 1)],
        unit * 320,
        room=ROOM,
    )
    node_pre, edge_pre = lax.optimization_barrier((node_pre, edge_pre))
    mesh_one, halo_box = call(
        functools.partial(mesh_body, count=len(totals)),
        [node_like, shape((halo_count, width))],
        totals + [nodes, node_pre, node_w, halo_hot, sent_w],
        unit * 1000,
    )
    ghosts = lax.all_to_all(
        halo_box.reshape(peers, -1, width), "patch", split_axis=0, concat_axis=0, tiled=True
    ).reshape(halo_count, width)
    edge_whole = shape((edge_total, width))
    edge_pre, node_pre = call(
        local_body,
        [edge_whole, node_like],
        [mesh_one, sent_w, Far(proc_edge_w, 2), Far(ends), Far(edge_pre), Far(proc_node_w, 0)],
        unit * 1500,
        far_outs=True,
        room=ROOM,
    )
    edge_operands = [Far(far), Far(ghosts), Far(edge_pre), Far(proc_edge_w, 3), Far(edges), Far(edge_recv)]
    node_operands = [Far(proc_node_w, 1, 2), Far(node_pre), Far(mesh_one)]
    if paired:
        edge_out, mesh_two = call(
            edge_node_body,
            [edge_like, node_like],
            edge_operands + node_operands,
            unit * 1500,
            far_outs=True,
            room=53.5,
        )
    else:
        edge_out, partial_two = call(
            edge_body, [edge_like, node_like], edge_operands, unit * 800, far_outs=True, room=BIG
        )
        (mesh_two,) = call(
            node_body,
            [node_like],
            [Far(band_sum(partial_two))] + node_operands,
            unit * 640,
            far_outs=True,
            room=BIG,
        )
    return (mesh_two, edge_out)


def solution(mesh):
    both = ("band", "patch")
    in_specs = (
        P(both, None),
        P(both),
        P(both, None),
        P(both),
        P(None, both),
        P("patch", None),
        P(both, None),
        P(both),
        P(both),
        P("patch", None),
        P(),
        P(),
        P(),
        P(),
        P(),
        P(),
        P(),
    )
    out_specs = (P("patch", None), P(both, None))
    return jax.shard_map(
        per_device, mesh=mesh, in_specs=in_specs, out_specs=out_specs, check_vma=False
    )
```

```python
import functools
import math

import jax
import jax.numpy as jnp
from jax import lax
from jax.experimental import pallas as pl
from jax.experimental.pallas import tpu as pltpu
from jax.sharding import PartitionSpec as P

F32 = jnp.float32
BF16 = jnp.bfloat16
LANES = 128
RADIX = 32


def dot_nn(left, right):
    return jnp.dot(left, right, preferred_element_type=F32)


def dot_nt(left, right):
    return lax.dot_general(left, right, (((1,), (1,)), ((), ())), preferred_element_type=F32)


def dot_tn(left, right):
    return lax.dot_general(left, right, (((0,), (0,)), ((), ())), preferred_element_type=F32)


def as_onehot(hits):
    return jnp.where(hits, 1.0, 0.0).astype(BF16)


def rows_equal(row_count, names):
    rows = lax.broadcasted_iota(jnp.int32, (row_count, names.shape[1]), 0)
    return as_onehot(rows == names)


def norm_rows(values_in):
    average = jnp.mean(values_in, axis=-1, keepdims=True)
    centred = values_in - average
    spread = jnp.mean(centred * centred, axis=-1, keepdims=True)
    return centred * lax.rsqrt(spread + 1e-05)


def silu(values_in):
    return values_in * jax.nn.sigmoid(values_in)


def tail(preact, out_weight):
    return norm_rows(dot_nn(silu(preact).astype(BF16), out_weight))


class Arriving:
    def __init__(self, source, held, sem):
        self.held, self.copy, self.waited = held, pltpu.make_async_copy(source, held, sem), False
        self.copy.start()

    def ref(self):
        if not self.waited:
            self.copy.wait()
            self.waited = True
        return self.held

    def __call__(self):
        return self.ref()[...]


class Present:
    def __init__(self, held):
        self.held = held

    def ref(self):
        return self.held

    def __call__(self):
        return self.held[...]


class Leaving:
    def __init__(self, held, target=None, sems=None):
        self.held, self.target, self.sems, self.copies = held, target, sems, []
        self.shape = held.shape

    def send(self, first, count):
        if self.target is not None:
            rows = pl.ds(first, count)
            copy = pltpu.make_async_copy(
                self.held.at[rows], self.target.at[rows], self.sems.at[len(self.copies)]
            )
            copy.start()
            self.copies.append(copy)

    def put(self, value, first=0):
        self.held[first : first + value.shape[0]] = value
        self.send(first, value.shape[0])


class Far:
    def __init__(self, array, index=None, count=None):
        self.array, self.index, self.count = array, index, count
        self.shape = array.shape
        if index is not None:
            self.shape = array.shape[1:] if count is None else (count,) + array.shape[1:]

    def source(self, ref):
        if self.index is None:
            return ref
        return ref.at[self.index if self.count is None else pl.ds(self.index, self.count)]


PARTS = 4
BIG, ROOM = 60, 48


def call(body, outs, operands, flops, far_outs=False, room=ROOM):
    n_in, n_out = len(operands), len(outs)
    far_in = [isinstance(operand, Far) for operand in operands]
    arrays = [operand.array if away else operand for operand, away in zip(operands, far_in)]
    moved = sum(math.prod(o.shape) * a.dtype.itemsize for o, a in zip(operands, arrays))

    def kernel(*refs):
        given, results, scratch = refs[:n_in], refs[n_in : n_in + n_out], list(refs[n_in + n_out : -2])
        in_sems, out_sems = refs[-2:]
        arriving = []
        for i, (ref, operand) in enumerate(zip(given, operands)):
            if far_in[i]:
                arriving.append(Arriving(operand.source(ref), scratch.pop(0), in_sems.at[i]))
            else:
                arriving.append(Present(ref))
        leaving = []
        for i, ref in enumerate(results):
            if far_outs:
                leaving.append(Leaving(scratch.pop(0), ref, out_sems.at[pl.ds(i * PARTS, PARTS)]))
            else:
                leaving.append(Leaving(ref))
        body(arriving, leaving)
        for one in leaving:
            for copy in one.copies:
                copy.wait()

    here, away = pl.BlockSpec(memory_space=pltpu.VMEM), pl.BlockSpec(memory_space=pltpu.HBM)
    held = [pltpu.VMEM(o.shape, a.dtype) for o, a, is_far in zip(operands, arrays, far_in) if is_far]
    if far_outs:
        held += [pltpu.VMEM(o.shape, o.dtype) for o in outs]
    return pl.pallas_call(
        kernel,
        in_specs=[away if is_far else here for is_far in far_in],
        out_specs=[away if far_outs else here] * n_out,
        out_shape=outs,
        scratch_shapes=held
        + [pltpu.SemaphoreType.DMA((n_in,)), pltpu.SemaphoreType.DMA((n_out * PARTS,))],
        compiler_params=pltpu.CompilerParams(vmem_limit_bytes=int(room * 1024) * 1024),
        cost_estimate=pl.CostEstimate(flops=flops, bytes_accessed=moved, transcendentals=0),
    )(*arrays)


def as_row(block):
    return jnp.concatenate([block[i : i + 1] for i in range(block.shape[0])], axis=1)


def embed_body(arriving, leaving):
    in_w, out_w, edge_w, feat, patch, sender, geo, node, geo_w = arriving
    (box,) = leaving
    peers, box_rows, _ = box.shape
    edges = patch.held.shape[1]
    grid_rows = feat.held.shape[1]
    pieces = edge_w.held.shape[1] // LANES
    capacity = 4 * edges // (3 * peers)
    slots = peers * capacity
    me = lax.axis_index("patch")
    earlier = as_onehot(
        lax.broadcasted_iota(jnp.int32, (edges, edges), 0)
        < lax.broadcasted_iota(jnp.int32, (edges, edges), 1)
    )
    patch = patch()
    named = lax.broadcasted_iota(jnp.int32, (peers, edges), 0) == patch
    named_f = jnp.where(named, 1.0, 0.0)
    before = dot_nn(named_f.astype(BF16), earlier)
    rank = jnp.sum(named_f * before, axis=0, keepdims=True).astype(jnp.int32)
    for one in arriving:
        one.ref()
    place = rows_equal(slots, patch * capacity + rank)
    source = rows_equal(grid_rows, as_row(sender()))
    pick = dot_nt(place, source).astype(BF16)
    geo = dot_nt(place, geo()).astype(BF16)

    address = as_row(node()) + 1
    first = me * capacity
    lane = rows_equal(LANES, rank + lax.rem(first, LANES))
    high = dot_nt((named_f * (address // RADIX).astype(F32)).astype(BF16), lane)
    low = dot_nt((named_f * lax.rem(address, RADIX).astype(F32)).astype(BF16), lane)
    extra = box_rows - pieces * capacity
    row = lax.broadcasted_iota(jnp.int32, (peers, extra, LANES), 1)
    mine = first // LANES
    words = jnp.where(
        row == mine,
        high[:, None, :],
        jnp.where(row == extra // 2 + mine, low[:, None, :], 0.0),
    )
    box.held[:, pieces * capacity :, :] = words.astype(BF16)

    hidden = silu(dot_tn(feat(), in_w())).astype(BF16)
    latent = norm_rows(dot_nn(hidden, out_w())).astype(BF16)
    rows = dot_nn(pick, latent).astype(BF16)
    some = peers // PARTS
    for part in range(PARTS):
        own = slice(part * some * capacity, (part + 1) * some * capacity)
        term = dot_nn(rows[own], edge_w()) + dot_nn(geo[own], geo_w())
        for piece in range(pieces):
            box.held[part * some : (part + 1) * some, piece * capacity : (piece + 1) * capacity, :] = (
                term[:, piece * LANES : (piece + 1) * LANES].reshape(some, capacity, LANES).astype(BF16)
            )
        box.send(part * some, some)


def edge_shadow_body(arriving, leaving, *, count):
    edge_parts, names, edge_w = arriving[:count], arriving[count:-1], arriving[-1]
    edges_out, pre_out, ends_out, far_out, recv_out = leaving
    size = edge_parts[0].held.shape[0]
    mesh_rows = ends_out.shape[1] // 2
    far_rows = far_out.shape[1]
    for part in range(count):
        rows = slice(part * size, (part + 1) * size)
        if count == 2:
            keep = lax.axis_index("band") == part
            send = jnp.where(keep, names[0](), names[2]()[0:1])
            recv = jnp.where(keep, names[1](), names[2]()[1:2])
            edges = jnp.where(keep, edge_parts[0](), edge_parts[1]())
        else:
            send, recv, edges = names[0](), names[1](), edge_parts[0]()
        recv_out.held[:, rows] = recv
        far_out.put(rows_equal(far_rows, send - mesh_rows).T, rows.start)
        ends = [rows_equal(mesh_rows, send).T, rows_equal(mesh_rows, recv).T]
        ends_out.put(jnp.concatenate(ends, axis=1), rows.start)
        edges_out.put(edges, rows.start)
        pre_out.put(dot_nn(edges, edge_w()).astype(BF16), rows.start)
    recv_out.send(0, 1)


def message_bring_body(arriving, leaving):
    nodes, recv_w, out_w = arriving
    (both,) = leaving
    both.put(dot_nn(nodes(), recv_w()).astype(BF16))
    both.put(out_w(), nodes.held.shape[0])


def mesh_bring_body(arriving, leaving):
    halo, nodes, node_w, pair_w, sent_w = arriving
    node_pre_out, halo_out, nodes_out, pair_w_out, sent_w_out = leaving
    halo_out.put(rows_equal(nodes.held.shape[0], halo()).T)
    nodes_out.put(nodes())
    node_pre_out.put(dot_nn(nodes(), node_w()).astype(BF16))
    pair_w_out.put(pair_w())
    sent_w_out.put(sent_w())


def message_body(arriving, leaving, *, capacity):
    box, both = arriving
    (total,) = leaving
    mesh_rows, width = total.shape
    peers = box.held.shape[0]
    pieces = width // LANES
    box = box.ref()
    words = jnp.sum(box[:, pieces * capacity :, :].astype(F32), axis=0)
    half = words.shape[0] // 2
    slots = peers * capacity
    hot = []
    for group in range(slots // LANES):
        name = words[group : group + 1] * float(RADIX) + words[half + group : half + group + 1] - 1.0
        hot.append(rows_equal(mesh_rows, name.astype(jnp.int32)))
    hot = jnp.concatenate(hot, axis=1)
    terms = jnp.concatenate(
        [
            box[:, piece * capacity : (piece + 1) * capacity, :].astype(F32).reshape(slots, LANES)
            for piece in range(pieces)
        ],
        axis=1,
    )
    message = tail(terms + dot_tn(hot, both.ref()[:mesh_rows]), both.ref()[mesh_rows:]).astype(BF16)
    total.put(dot_nn(hot, message).astype(BF16))


def mesh_body(arriving, leaving, *, count):
    totals, (nodes, node_pre, pair_w, halo_hot, sent_w) = arriving[:count], arriving[count:]
    one_out, box_out = leaving
    total = totals[0]().astype(F32)
    for other in totals[1:]:
        total = total + other().astype(F32)
    preact = node_pre().astype(F32) + dot_nn(total.astype(BF16), pair_w.ref()[0])
    one = (nodes().astype(F32) + tail(preact, pair_w.ref()[1])).astype(BF16)
    one_out.put(one)
    rows = dot_nn(halo_hot(), one).astype(BF16)
    box_out.put(dot_nn(rows, sent_w()).astype(BF16))


def local_body(arriving, leaving):
    one, sent_w, recv_w, ends, pre, node_w = arriving
    pre_out, node_pre_out = leaving
    sent = dot_nn(one(), sent_w()).astype(BF16)
    recv = dot_nn(one(), recv_w()).astype(BF16)
    own = dot_nn(ends(), jnp.concatenate([sent, recv], axis=0))
    pre_out.put((pre().astype(F32) + own).astype(BF16))
    node_pre_out.put(dot_nn(one(), node_w()).astype(BF16))


def edge_values(arriving):
    far, ghosts, pre, edge_w, edges = arriving
    preact = dot_nn(far(), ghosts()) + pre().astype(F32)
    return (edges().astype(F32) + tail(preact, edge_w())).astype(BF16)


def node_values(total, arriving):
    pair_w, node_pre, one = arriving
    preact = node_pre().astype(F32) + dot_nn(total, pair_w.ref()[0])
    return (one().astype(F32) + tail(preact, pair_w.ref()[1])).astype(BF16)


def edge_node_body(arriving, leaving):
    edge_out, two_out = leaving
    made = edge_values(arriving[:5])
    size = edge_out.shape[0]
    edge_out.put(jnp.where(lax.axis_index("band") == 0, made[:size], made[size:]))
    target = rows_equal(two_out.shape[0], arriving[5]())
    two_out.put(node_values(dot_nn(target, made).astype(BF16), arriving[6:]))


def edge_body(arriving, leaving):
    edge_out, total_out = leaving
    made = edge_values(arriving[:5])
    edge_out.put(made)
    total_out.put(dot_nn(rows_equal(total_out.shape[0], arriving[5]()), made).astype(BF16))


def node_body(arriving, leaving):
    leaving[0].put(node_values(arriving[0](), arriving[1:]))


def shape(dims, dtype=BF16):
    return jax.ShapeDtypeStruct(dims, dtype)


def per_device(
    grid_feat,
    enc_sender,
    enc_patch,
    enc_node,
    enc_geo,
    mesh_nodes,
    mesh_edge,
    mesh_send,
    mesh_recv,
    halo_rows,
    grid_in,
    grid_out,
    geo_weight,
    enc_edge_w,
    enc_node_w,
    proc_edge_w,
    proc_node_w,
):
    bands, peers = lax.axis_size("band"), lax.axis_size("patch")
    mesh_count, width = mesh_nodes.shape
    edge_count, medge_count = enc_sender.shape[0], mesh_edge.shape[0]
    halo_count = halo_rows.shape[1]
    capacity = 4 * edge_count // (3 * peers)
    slots = peers * capacity
    pieces = width // LANES
    address_rows = 2 * (slots // LANES)
    paired = bands == 2
    other = [(0, 1), (1, 0)]
    unit = 2 * width * width

    def band_sum(partial_value):
        share = lax.psum_scatter(partial_value, "band", scatter_dimension=0, tiled=True)
        return lax.all_gather(share, "band", axis=0, tiled=True)

    matrix, pair = shape((width, width)), shape((2, width, width))
    node_like, edge_like = shape((mesh_count, width)), shape((medge_count, width))
    sources = [
        grid_feat.T,
        enc_patch.reshape(1, -1),
        enc_sender.reshape(-1, LANES),
        enc_geo,
        enc_node.reshape(-1, LANES),
        geo_weight,
    ]
    (outbox,) = call(
        embed_body,
        [shape((peers, pieces * capacity + address_rows, LANES))],
        [Far(grid_in), Far(grid_out), Far(enc_edge_w, 0)] + [Far(source) for source in sources],
        unit * 1500,
        far_outs=True,
        room=BIG,
    )
    inbox = lax.all_to_all(outbox, "patch", split_axis=0, concat_axis=0, tiled=True)

    send_row, recv_row = mesh_send.reshape(1, -1), mesh_recv.reshape(1, -1)
    edge_parts, names = [mesh_edge], [send_row, recv_row]
    if paired:
        own_edge, own_names, _ = lax.optimization_barrier(
            (mesh_edge, jnp.concatenate(names, axis=0), outbox)
        )
        edge_parts.append(lax.ppermute(own_edge, "band", other))
        names.append(lax.ppermute(own_names, "band", other))
    count = len(edge_parts)
    edge_total = count * medge_count
    nodes, _ = lax.optimization_barrier((mesh_nodes, outbox))
    (message_pair,) = call(
        message_bring_body,
        [shape((mesh_count + width, width))],
        [Far(nodes), Far(enc_edge_w, 1), Far(enc_edge_w, 2)],
        unit * 320,
        room=ROOM,
    )
    message_pair, edge_parts[-1], names[-1] = lax.optimization_barrier(
        (message_pair, edge_parts[-1], names[-1])
    )
    (partial_value,) = call(
        functools.partial(message_body, capacity=capacity),
        [node_like],
        [inbox, message_pair],
        unit * 1200,
    )
    names[0], partial_value = lax.optimization_barrier((names[0], partial_value))
    edges, edge_pre, ends, far, edge_recv = call(
        functools.partial(edge_shadow_body, count=count),
        [
            shape((edge_total, width)),
            shape((edge_total, width)),
            shape((edge_total, 2 * mesh_count)),
            shape((edge_total, halo_count)),
            shape((1, edge_total), jnp.int32),
        ],
        [Far(one) for one in edge_parts + names] + [Far(proc_edge_w, 0)],
        unit * edge_total,
        far_outs=True,
        room=ROOM,
    )
    if paired:
        totals = [partial_value, lax.ppermute(partial_value, "band", other)]
    else:
        totals = [band_sum(partial_value)]
    nodes, halo_rows, _ = lax.optimization_barrier((mesh_nodes, halo_rows, partial_value))
    node_pre, halo_hot, nodes, node_w, sent_w = call(
        mesh_bring_body,
        [node_like, shape((halo_count, mesh_count)), node_like, pair, matrix],
        [Far(halo_rows), Far(nodes), Far(enc_node_w, 0), Far(enc_node_w, 1, 2), Far(proc_edge_w, 1)],
        unit * 320,
        room=ROOM,
    )
    node_pre, edge_pre = lax.optimization_barrier((node_pre, edge_pre))
    mesh_one, halo_box = call(
        functools.partial(mesh_body, count=len(totals)),
        [node_like, shape((halo_count, width))],
        totals + [nodes, node_pre, node_w, halo_hot, sent_w],
        unit * 1000,
    )
    ghosts = lax.all_to_all(
        halo_box.reshape(peers, -1, width), "patch", split_axis=0, concat_axis=0, tiled=True
    ).reshape(halo_count, width)
    edge_whole = shape((edge_total, width))
    edge_pre, node_pre = call(
        local_body,
        [edge_whole, node_like],
        [mesh_one, sent_w, Far(proc_edge_w, 2), Far(ends), Far(edge_pre), Far(proc_node_w, 0)],
        unit * 1500,
        far_outs=True,
        room=ROOM,
    )
    edge_operands = [Far(far), Far(ghosts), Far(edge_pre), Far(proc_edge_w, 3), Far(edges), Far(edge_recv)]
    node_operands = [Far(proc_node_w, 1, 2), Far(node_pre), Far(mesh_one)]
    if paired:
        edge_out, mesh_two = call(
            edge_node_body,
            [edge_like, node_like],
            edge_operands + node_operands,
            unit * 1500,
            far_outs=True,
            room=53.5,
        )
    else:
        edge_out, partial_two = call(
            edge_body, [edge_like, node_like], edge_operands, unit * 800, far_outs=True, room=BIG
        )
        (mesh_two,) = call(
            node_body,
            [node_like],
            [Far(band_sum(partial_two))] + node_operands,
            unit * 640,
            far_outs=True,
            room=BIG,
        )
    return (mesh_two, edge_out)


def solution(mesh):
    both = ("band", "patch")
    in_specs = (
        P(both, None),
        P(both),
        P(both, None),
        P(both),
        P(None, both),
        P("patch", None),
        P(both, None),
        P(both),
        P(both),
        P("patch", None),
        P(),
        P(),
        P(),
        P(),
        P(),
        P(),
        P(),
    )
    out_specs = (P("patch", None), P(both, None))
    return jax.shard_map(
        per_device, mesh=mesh, in_specs=in_specs, out_specs=out_specs, check_vma=False
    )
```

```python
import functools
import math

import jax
import jax.numpy as jnp
from jax import lax
from jax.experimental import pallas as pl
from jax.experimental.pallas import tpu as pltpu
from jax.sharding import PartitionSpec as P

F32 = jnp.float32
BF16 = jnp.bfloat16
LANES = 128
RADIX = 32


def dot_nn(left, right):
    return jnp.dot(left, right, preferred_element_type=F32)


def dot_nt(left, right):
    return lax.dot_general(left, right, (((1,), (1,)), ((), ())), preferred_element_type=F32)


def dot_tn(left, right):
    return lax.dot_general(left, right, (((0,), (0,)), ((), ())), preferred_element_type=F32)


def as_onehot(hits):
    return jnp.where(hits, 1.0, 0.0).astype(BF16)


def rows_equal(row_count, names):
    rows = lax.broadcasted_iota(jnp.int32, (row_count, names.shape[1]), 0)
    return as_onehot(rows == names)


def norm_rows(values_in):
    average = jnp.mean(values_in, axis=-1, keepdims=True)
    centred = values_in - average
    spread = jnp.mean(centred * centred, axis=-1, keepdims=True)
    return centred * lax.rsqrt(spread + 1e-05)


def silu(values_in):
    return values_in * jax.nn.sigmoid(values_in)


def centre(weight):
    wide = weight.astype(F32)
    return (wide - jnp.mean(wide, axis=-1, keepdims=True)).astype(BF16)


def tail(preact, centred_weight):
    centred = dot_nn(silu(preact).astype(BF16), centred_weight)
    spread = jnp.mean(centred * centred, axis=-1, keepdims=True)
    return centred * lax.rsqrt(spread + 1e-05)


class Arriving:
    def __init__(self, source, held, sem):
        self.held, self.copy, self.waited = held, pltpu.make_async_copy(source, held, sem), False
        self.copy.start()

    def ref(self):
        if not self.waited:
            self.copy.wait()
            self.waited = True
        return self.held

    def __call__(self):
        return self.ref()[...]


class Present:
    def __init__(self, held):
        self.held = held

    def ref(self):
        return self.held

    def __call__(self):
        return self.held[...]


class Leaving:
    def __init__(self, held, target=None, sems=None):
        self.held, self.target, self.sems, self.copies = held, target, sems, []
        self.shape = held.shape

    def send(self, first, count):
        if self.target is not None:
            rows = pl.ds(first, count)
            copy = pltpu.make_async_copy(
                self.held.at[rows], self.target.at[rows], self.sems.at[len(self.copies)]
            )
            copy.start()
            self.copies.append(copy)

    def put(self, value, first=0):
        self.held[first : first + value.shape[0]] = value
        self.send(first, value.shape[0])


class Far:
    def __init__(self, array, index=None, count=None):
        self.array, self.index, self.count = array, index, count
        self.shape = array.shape
        if index is not None:
            self.shape = array.shape[1:] if count is None else (count,) + array.shape[1:]

    def source(self, ref):
        if self.index is None:
            return ref
        return ref.at[self.index if self.count is None else pl.ds(self.index, self.count)]


PARTS = 4
BIG, ROOM = 60, 48


def call(body, outs, operands, flops, far_outs=False, room=ROOM):
    n_in, n_out = len(operands), len(outs)
    far_in = [isinstance(operand, Far) for operand in operands]
    arrays = [operand.array if away else operand for operand, away in zip(operands, far_in)]
    moved = sum(math.prod(o.shape) * a.dtype.itemsize for o, a in zip(operands, arrays))

    def kernel(*refs):
        given, results, scratch = refs[:n_in], refs[n_in : n_in + n_out], list(refs[n_in + n_out : -2])
        in_sems, out_sems = refs[-2:]
        arriving = []
        for i, (ref, operand) in enumerate(zip(given, operands)):
            if far_in[i]:
                arriving.append(Arriving(operand.source(ref), scratch.pop(0), in_sems.at[i]))
            else:
                arriving.append(Present(ref))
        leaving = []
        for i, ref in enumerate(results):
            if far_outs:
                leaving.append(Leaving(scratch.pop(0), ref, out_sems.at[pl.ds(i * PARTS, PARTS)]))
            else:
                leaving.append(Leaving(ref))
        body(arriving, leaving)
        for one in leaving:
            for copy in one.copies:
                copy.wait()

    here, away = pl.BlockSpec(memory_space=pltpu.VMEM), pl.BlockSpec(memory_space=pltpu.HBM)
    held = [pltpu.VMEM(o.shape, a.dtype) for o, a, is_far in zip(operands, arrays, far_in) if is_far]
    if far_outs:
        held += [pltpu.VMEM(o.shape, o.dtype) for o in outs]
    return pl.pallas_call(
        kernel,
        in_specs=[away if is_far else here for is_far in far_in],
        out_specs=[away if far_outs else here] * n_out,
        out_shape=outs,
        scratch_shapes=held
        + [pltpu.SemaphoreType.DMA((n_in,)), pltpu.SemaphoreType.DMA((n_out * PARTS,))],
        compiler_params=pltpu.CompilerParams(vmem_limit_bytes=int(room * 1024) * 1024),
        cost_estimate=pl.CostEstimate(flops=flops, bytes_accessed=moved, transcendentals=0),
    )(*arrays)


def as_row(block):
    return jnp.concatenate([block[i : i + 1] for i in range(block.shape[0])], axis=1)


def embed_body(arriving, leaving):
    in_w, out_w, edge_w, feat, patch, sender, geo, node, geo_w = arriving
    (box,) = leaving
    peers, box_rows, _ = box.shape
    edges = patch.held.shape[1]
    grid_rows = feat.held.shape[1]
    pieces = edge_w.held.shape[1] // LANES
    capacity = 4 * edges // (3 * peers)
    slots = peers * capacity
    me = lax.axis_index("patch")
    earlier = as_onehot(
        lax.broadcasted_iota(jnp.int32, (edges, edges), 0)
        < lax.broadcasted_iota(jnp.int32, (edges, edges), 1)
    )
    patch = patch()
    named = lax.broadcasted_iota(jnp.int32, (peers, edges), 0) == patch
    named_f = jnp.where(named, 1.0, 0.0)
    before = dot_nn(named_f.astype(BF16), earlier)
    rank = jnp.sum(named_f * before, axis=0, keepdims=True).astype(jnp.int32)
    for one in arriving:
        one.ref()
    place = rows_equal(slots, patch * capacity + rank)
    source = rows_equal(grid_rows, as_row(sender()))
    pick = dot_nt(place, source).astype(BF16)
    geo = dot_nt(place, geo()).astype(BF16)

    address = as_row(node()) + 1
    first = me * capacity
    lane = rows_equal(LANES, rank + lax.rem(first, LANES))
    high = dot_nt((named_f * (address // RADIX).astype(F32)).astype(BF16), lane)
    low = dot_nt((named_f * lax.rem(address, RADIX).astype(F32)).astype(BF16), lane)
    extra = box_rows - pieces * capacity
    row = lax.broadcasted_iota(jnp.int32, (peers, extra, LANES), 1)
    mine = first // LANES
    words = jnp.where(
        row == mine,
        high[:, None, :],
        jnp.where(row == extra // 2 + mine, low[:, None, :], 0.0),
    )
    box.held[:, pieces * capacity :, :] = words.astype(BF16)

    hidden = silu(dot_tn(feat(), in_w())).astype(BF16)
    latent = norm_rows(dot_nn(hidden, out_w())).astype(BF16)
    rows = dot_nn(pick, latent).astype(BF16)
    some = peers // PARTS
    for part in range(PARTS):
        own = slice(part * some * capacity, (part + 1) * some * capacity)
        term = dot_nn(rows[own], edge_w()) + dot_nn(geo[own], geo_w())
        for piece in range(pieces):
            box.held[part * some : (part + 1) * some, piece * capacity : (piece + 1) * capacity, :] = (
                term[:, piece * LANES : (piece + 1) * LANES].reshape(some, capacity, LANES).astype(BF16)
            )
        box.send(part * some, some)


def edge_shadow_body(arriving, leaving, *, count):
    edge_parts, names, edge_w = arriving[:count], arriving[count:-1], arriving[-1]
    edges_out, pre_out, ends_out, far_out, recv_out = leaving
    size = edge_parts[0].held.shape[0]
    mesh_rows = ends_out.shape[1] // 2
    far_rows = far_out.shape[1]
    for part in range(count):
        rows = slice(part * size, (part + 1) * size)
        if count == 2:
            keep = lax.axis_index("band") == part
            send = jnp.where(keep, names[0](), names[2]()[0:1])
            recv = jnp.where(keep, names[1](), names[2]()[1:2])
            edges = jnp.where(keep, edge_parts[0](), edge_parts[1]())
        else:
            send, recv, edges = names[0](), names[1](), edge_parts[0]()
        recv_out.held[:, rows] = recv
        far_out.put(rows_equal(far_rows, send - mesh_rows).T, rows.start)
        ends = [rows_equal(mesh_rows, send).T, rows_equal(mesh_rows, recv).T]
        ends_out.put(jnp.concatenate(ends, axis=1), rows.start)
        edges_out.put(edges, rows.start)
        pre_out.put(dot_nn(edges, edge_w()).astype(BF16), rows.start)
    recv_out.send(0, 1)


def message_bring_body(arriving, leaving):
    nodes, recv_w, out_w = arriving
    (both,) = leaving
    both.put(dot_nn(nodes(), recv_w()).astype(BF16))
    both.put(centre(out_w()), nodes.held.shape[0])


def mesh_bring_body(arriving, leaving):
    halo, nodes, node_w, pair_w, sent_w = arriving
    node_pre_out, halo_out, nodes_out, pair_w_out, sent_w_out = leaving
    halo_out.put(rows_equal(nodes.held.shape[0], halo()).T)
    nodes_out.put(nodes())
    node_pre_out.put(dot_nn(nodes(), node_w()).astype(BF16))
    pair_w_out.held[0] = pair_w.ref()[0]
    pair_w_out.held[1] = centre(pair_w.ref()[1])
    sent_w_out.put(sent_w())


def message_body(arriving, leaving, *, capacity):
    box, both = arriving
    (total,) = leaving
    mesh_rows, width = total.shape
    peers = box.held.shape[0]
    pieces = width // LANES
    box = box.ref()
    words = jnp.sum(box[:, pieces * capacity :, :].astype(F32), axis=0)
    half = words.shape[0] // 2
    slots = peers * capacity
    hot = []
    for group in range(slots // LANES):
        name = words[group : group + 1] * float(RADIX) + words[half + group : half + group + 1] - 1.0
        hot.append(rows_equal(mesh_rows, name.astype(jnp.int32)))
    hot = jnp.concatenate(hot, axis=1)
    terms = jnp.concatenate(
        [
            box[:, piece * capacity : (piece + 1) * capacity, :].astype(F32).reshape(slots, LANES)
            for piece in range(pieces)
        ],
        axis=1,
    )
    message = tail(terms + dot_tn(hot, both.ref()[:mesh_rows]), both.ref()[mesh_rows:]).astype(BF16)
    total.put(dot_nn(hot, message).astype(BF16))


def mesh_body(arriving, leaving, *, count):
    totals, (nodes, node_pre, pair_w, halo_hot, sent_w) = arriving[:count], arriving[count:]
    one_out, box_out = leaving
    total = totals[0]().astype(F32)
    for other in totals[1:]:
        total = total + other().astype(F32)
    preact = node_pre().astype(F32) + dot_nn(total.astype(BF16), pair_w.ref()[0])
    one = (nodes().astype(F32) + tail(preact, pair_w.ref()[1])).astype(BF16)
    one_out.put(one)
    rows = dot_nn(halo_hot(), one).astype(BF16)
    box_out.put(dot_nn(rows, sent_w()).astype(BF16))


def local_body(arriving, leaving):
    one, sent_w, recv_w, ends, pre, node_w, edge_out_w, node_out_w = arriving
    pre_out, node_pre_out, edge_centred, node_centred = leaving
    sent = dot_nn(one(), sent_w()).astype(BF16)
    recv = dot_nn(one(), recv_w()).astype(BF16)
    own = dot_nn(ends(), jnp.concatenate([sent, recv], axis=0))
    pre_out.put((pre().astype(F32) + own).astype(BF16))
    node_pre_out.put(dot_nn(one(), node_w()).astype(BF16))
    edge_centred.put(centre(edge_out_w()))
    node_centred.put(centre(node_out_w()))


def edge_values(arriving):
    far, ghosts, pre, edge_w, edges = arriving
    preact = dot_nn(far(), ghosts()) + pre().astype(F32)
    return (edges().astype(F32) + tail(preact, edge_w())).astype(BF16)


def node_values(total, arriving):
    sum_w, node_pre, out_w, one = arriving
    preact = node_pre().astype(F32) + dot_nn(total, sum_w())
    return (one().astype(F32) + tail(preact, out_w())).astype(BF16)


def edge_node_body(arriving, leaving):
    edge_out, two_out = leaving
    made = edge_values(arriving[:5])
    size = edge_out.shape[0]
    edge_out.put(jnp.where(lax.axis_index("band") == 0, made[:size], made[size:]))
    target = rows_equal(two_out.shape[0], arriving[5]())
    two_out.put(node_values(dot_nn(target, made).astype(BF16), arriving[6:]))


def edge_body(arriving, leaving):
    edge_out, total_out = leaving
    made = edge_values(arriving[:5])
    edge_out.put(made)
    total_out.put(dot_nn(rows_equal(total_out.shape[0], arriving[5]()), made).astype(BF16))


def node_body(arriving, leaving):
    leaving[0].put(node_values(arriving[0](), arriving[1:]))


def shape(dims, dtype=BF16):
    return jax.ShapeDtypeStruct(dims, dtype)


def per_device(
    grid_feat,
    enc_sender,
    enc_patch,
    enc_node,
    enc_geo,
    mesh_nodes,
    mesh_edge,
    mesh_send,
    mesh_recv,
    halo_rows,
    grid_in,
    grid_out,
    geo_weight,
    enc_edge_w,
    enc_node_w,
    proc_edge_w,
    proc_node_w,
):
    bands, peers = lax.axis_size("band"), lax.axis_size("patch")
    mesh_count, width = mesh_nodes.shape
    edge_count, medge_count = enc_sender.shape[0], mesh_edge.shape[0]
    halo_count = halo_rows.shape[1]
    capacity = 4 * edge_count // (3 * peers)
    slots = peers * capacity
    pieces = width // LANES
    address_rows = 2 * (slots // LANES)
    paired = bands == 2
    other = [(0, 1), (1, 0)]
    unit = 2 * width * width

    def band_sum(partial_value):
        share = lax.psum_scatter(partial_value, "band", scatter_dimension=0, tiled=True)
        return lax.all_gather(share, "band", axis=0, tiled=True)

    matrix, pair = shape((width, width)), shape((2, width, width))
    node_like, edge_like = shape((mesh_count, width)), shape((medge_count, width))
    sources = [
        grid_feat.T,
        enc_patch.reshape(1, -1),
        enc_sender.reshape(-1, LANES),
        enc_geo,
        enc_node.reshape(-1, LANES),
        geo_weight,
    ]
    (outbox,) = call(
        embed_body,
        [shape((peers, pieces * capacity + address_rows, LANES))],
        [Far(grid_in), Far(grid_out), Far(enc_edge_w, 0)] + [Far(source) for source in sources],
        unit * 1500,
        far_outs=True,
        room=BIG,
    )
    inbox = lax.all_to_all(outbox, "patch", split_axis=0, concat_axis=0, tiled=True)

    send_row, recv_row = mesh_send.reshape(1, -1), mesh_recv.reshape(1, -1)
    edge_parts, names = [mesh_edge], [send_row, recv_row]
    if paired:
        own_edge, own_names, _ = lax.optimization_barrier(
            (mesh_edge, jnp.concatenate(names, axis=0), outbox)
        )
        edge_parts.append(lax.ppermute(own_edge, "band", other))
        names.append(lax.ppermute(own_names, "band", other))
    count = len(edge_parts)
    edge_total = count * medge_count
    nodes, _ = lax.optimization_barrier((mesh_nodes, outbox))
    (message_pair,) = call(
        message_bring_body,
        [shape((mesh_count + width, width))],
        [Far(nodes), Far(enc_edge_w, 1), Far(enc_edge_w, 2)],
        unit * 320,
        room=ROOM,
    )
    message_pair, edge_parts[-1], names[-1] = lax.optimization_barrier(
        (message_pair, edge_parts[-1], names[-1])
    )
    (partial_value,) = call(
        functools.partial(message_body, capacity=capacity),
        [node_like],
        [inbox, message_pair],
        unit * 1200,
    )
    names[0], partial_value = lax.optimization_barrier((names[0], partial_value))
    edges, edge_pre, ends, far, edge_recv = call(
        functools.partial(edge_shadow_body, count=count),
        [
            shape((edge_total, width)),
            shape((edge_total, width)),
            shape((edge_total, 2 * mesh_count)),
            shape((edge_total, halo_count)),
            shape((1, edge_total), jnp.int32),
        ],
        [Far(one) for one in edge_parts + names] + [Far(proc_edge_w, 0)],
        unit * edge_total,
        far_outs=True,
        room=ROOM,
    )
    if paired:
        totals = [partial_value, lax.ppermute(partial_value, "band", other)]
    else:
        totals = [band_sum(partial_value)]
    nodes, halo_rows, _ = lax.optimization_barrier((mesh_nodes, halo_rows, partial_value))
    node_pre, halo_hot, nodes, node_w, sent_w = call(
        mesh_bring_body,
        [node_like, shape((halo_count, mesh_count)), node_like, pair, matrix],
        [Far(halo_rows), Far(nodes), Far(enc_node_w, 0), Far(enc_node_w, 1, 2), Far(proc_edge_w, 1)],
        unit * 320,
        room=ROOM,
    )
    node_pre, edge_pre = lax.optimization_barrier((node_pre, edge_pre))
    mesh_one, halo_box = call(
        functools.partial(mesh_body, count=len(totals)),
        [node_like, shape((halo_count, width))],
        totals + [nodes, node_pre, node_w, halo_hot, sent_w],
        unit * 1000,
    )
    ghosts = lax.all_to_all(
        halo_box.reshape(peers, -1, width), "patch", split_axis=0, concat_axis=0, tiled=True
    ).reshape(halo_count, width)
    edge_whole = shape((edge_total, width))
    edge_pre, node_pre, edge_centred, node_centred = call(
        local_body,
        [edge_whole, node_like, matrix, matrix],
        [mesh_one, sent_w, Far(proc_edge_w, 2), Far(ends), Far(edge_pre), Far(proc_node_w, 0)]
        + [Far(proc_edge_w, 3), Far(proc_node_w, 2)],
        unit * 1500,
        far_outs=True,
        room=ROOM,
    )
    edge_operands = [Far(far), Far(ghosts), Far(edge_pre), Far(edge_centred), Far(edges), Far(edge_recv)]
    node_operands = [Far(proc_node_w, 1), Far(node_pre), Far(node_centred), Far(mesh_one)]
    if paired:
        edge_out, mesh_two = call(
            edge_node_body,
            [edge_like, node_like],
            edge_operands + node_operands,
            unit * 1500,
            far_outs=True,
            room=53.5,
        )
    else:
        edge_out, partial_two = call(
            edge_body, [edge_like, node_like], edge_operands, unit * 800, far_outs=True, room=BIG
        )
        (mesh_two,) = call(
            node_body,
            [node_like],
            [Far(band_sum(partial_two))] + node_operands,
            unit * 640,
            far_outs=True,
            room=BIG,
        )
    return (mesh_two, edge_out)


def solution(mesh):
    both = ("band", "patch")
    in_specs = (
        P(both, None),
        P(both),
        P(both, None),
        P(both),
        P(None, both),
        P("patch", None),
        P(both, None),
        P(both),
        P(both),
        P("patch", None),
        P(),
        P(),
        P(),
        P(),
        P(),
        P(),
        P(),
    )
    out_specs = (P("patch", None), P(both, None))
    return jax.shard_map(
        per_device, mesh=mesh, in_specs=in_specs, out_specs=out_specs, check_vma=False
    )
```
